32 devices in a mesh: row: 8 (over z, y), col: 4 (over x, core).
Axes of the slice: x: 2, y: 2, z: 4, core: 2. Of those that a mesh axis runs over, the one named last changes fastest.
Arguments:
- matrix: bfloat16 [28672, 28672], P('row', 'col'), may hold values from -1.5 to 16, as said below
Outputs:
- factored: bfloat16 [28672, 28672], P('row', 'col')
The draws below stay inside these ranges and needn't reach their ends.
Inputs may be any that keep to these rules, and one draw needn't show every extreme that they name: `matrix`: in logical order, diagonal entries lie between 12 and 16 and off-diagonal entries have magnitude at most 1.5.
All inputs are finite; a program needn't handle non-finite values.
Results may differ from the reference program's by a relative error of at most 0.0025.
The reference program's roundings to bfloat16 on the way count: a program that leaves them out, or rounds other values in their place, can miss the bound.
Values may be sent and summed in bfloat16 or wider, within the bound.
No kernel may reach another device: no remote copies, remote signals or barrier semaphores. Data moves between devices by JAX's collectives and lax.ppermute only.
A program may use at most 384 MiB of HBM per device.

```python
import jax
import jax.numpy as jnp
from jax import lax

N = 28672
NB = 256
STEPS = 2
N_ROW = 8
N_COL = 4


def draw_matrix(key, part):
    key_off = jax.random.fold_in(key, 11)
    key_diag = jax.random.fold_in(key, 12)
    key_front = jax.random.fold_in(key, 13)
    off_diag = jnp.clip(jax.random.normal(key_off, (N, N), jnp.float32) * 0.25, -1.5, 1.5)
    diag_values = jax.random.uniform(key_diag, (N,), jnp.float32, 12.0, 16.0)
    front_values = jax.random.uniform(key_front, (N, N), jnp.float32, 0.0, 1.5)
    stored = jnp.arange(N, dtype=jnp.int32)
    row_len = N // N_ROW
    col_len = N // N_COL
    row_logical = (stored % row_len // NB * N_ROW + stored // row_len) * NB + stored % NB
    col_logical = (stored % col_len // NB * N_COL + stored // col_len) * NB + stored % NB
    row_panel = row_logical // NB
    col_panel = col_logical // NB
    in_front = (row_panel[:, None] == col_panel[None, :]) & (row_panel[:, None] < STEPS)
    off_diag = jnp.where(in_front, front_values, off_diag)
    full = jnp.where(row_logical[:, None] == col_logical[None, :], diag_values[row_logical][:, None], off_diag)
    return full.astype(jnp.bfloat16)


def setup_inputs(seed: int = 0) -> dict:
    key_of = jax.random.split(jax.random.key(seed), 2)
    matrix = draw_matrix(jax.random.fold_in(key_of[1], 71), 0)
    return dict(matrix=matrix)


def factor_block(block):
    work = block.astype(jnp.float32)
    size = work.shape[0]
    positions = jnp.arange(size, dtype=jnp.int32)

    def eliminate(column, work):
        values = lax.dynamic_slice_in_dim(work, column, 1, 1)[:, 0]
        pivot_row = lax.dynamic_slice_in_dim(work, column, 1, 0)[0]
        pivot = jnp.sum(jnp.where(positions == column, pivot_row, 0.0))
        scaled = jnp.where(positions > column, values / pivot, 0.0)
        across = jnp.where(positions > column, pivot_row, 0.0)
        work = work - scaled[:, None] * across[None, :]
        kept = jnp.where(positions > column, scaled, values)
        return jnp.where(positions[None, :] == column, kept[:, None], work)

    return lax.fori_loop(0, size, eliminate, work)


def invert_upper(upper):
    size = upper.shape[0]
    positions = jnp.arange(size, dtype=jnp.int32)

    def substitute(count, inverse):
        index = (size - 1 - count)
        line = lax.dynamic_slice_in_dim(upper, index, 1, 0)[0]
        strict = jnp.where(positions > index, line, 0.0)
        pivot = jnp.sum(jnp.where(positions == index, line, 0.0))
        unit = jnp.where(positions == index, 1.0, 0.0).astype(jnp.float32)
        fresh = (unit - jnp.dot(strict, inverse, precision=lax.Precision.HIGHEST)) / pivot
        return jnp.where(positions[:, None] == index, fresh[None, :], inverse)

    return lax.fori_loop(0, size, substitute, jnp.zeros((size, size), jnp.float32))


def invert_lower(lower):
    size = lower.shape[0]
    positions = jnp.arange(size, dtype=jnp.int32)

    def substitute(index, inverse):
        line = lax.dynamic_slice_in_dim(lower, index, 1, 0)[0]
        strict = jnp.where(positions < index, line, 0.0)
        unit = jnp.where(positions == index, 1.0, 0.0).astype(jnp.float32)
        fresh = unit - jnp.dot(strict, inverse, precision=lax.Precision.HIGHEST)
        return jnp.where(positions[:, None] == index, fresh[None, :], inverse)

    return lax.fori_loop(0, size, substitute, jnp.zeros((size, size), jnp.float32))


def to_logical(stored):
    shaped = stored.reshape(N_ROW, N // N_ROW // NB, NB, N_COL, N // N_COL // NB, NB)
    return shaped.transpose(1, 0, 2, 4, 3, 5).reshape(N, N)


def to_stored(logical):
    shaped = logical.reshape(N // N_ROW // NB, N_ROW, NB, N // N_COL // NB, N_COL, NB)
    return shaped.transpose(1, 0, 2, 4, 3, 5).reshape(N, N)


def reference(matrix):
    work = to_logical(matrix)
    for section in range(STEPS):
        start = section * NB
        finish = start + NB
        packed = factor_block(work[start:finish, start:finish])
        upper = jnp.triu(packed)
        lower = jnp.tril(packed, -1) + jnp.eye(NB, dtype=packed.dtype)
        upper_inverse = invert_upper(upper)
        lower_inverse = invert_lower(lower)
        below = work[finish:, start:finish].astype(jnp.float32)
        left_panel = jnp.dot(below, upper_inverse, precision=lax.Precision.HIGHEST).astype(jnp.bfloat16)
        right = work[start:finish, finish:].astype(jnp.float32)
        top_panel = jnp.dot(lower_inverse, right, precision=lax.Precision.HIGHEST).astype(jnp.bfloat16)
        pieces = []
        for first in range(finish, N, 4096):
            last = min(first + 4096, N)
            update = jnp.dot(left_panel[first - finish:last - finish], top_panel, preferred_element_type=jnp.float32)
            pieces.append((work[first:last, finish:].astype(jnp.float32) - update).astype(jnp.bfloat16))
        work = work.at[start:finish, start:finish].set(packed.astype(jnp.bfloat16))
        work = work.at[finish:, start:finish].set(left_panel)
        work = work.at[start:finish, finish:].set(top_panel)
        work = work.at[finish:, finish:].set(jnp.concatenate(pieces, axis=0))
    return to_stored(work)
```

```python
import functools

import jax
import jax.numpy as jnp
from jax import lax
from jax.experimental import pallas as pl
from jax.experimental.pallas import tpu as pltpu
from jax.sharding import PartitionSpec as P

NB = 256
W = 32
MICRO = 4
CHUNKS = 14
DELAY = 2
PIECES = 4
FIRST_PIECE = 4
BATCHES = ((0, 4), (4, 7), (7, 10), (10, 12), (12, 14))
LIMIT = 56 * 2**20


def split3(x):
    high = x.astype(jnp.bfloat16)
    rest = x - high.astype(jnp.float32)
    middle = rest.astype(jnp.bfloat16)
    low = (rest - middle.astype(jnp.float32)).astype(jnp.bfloat16)
    return high, middle, low


def dot(a, b):
    return jnp.dot(a, b, preferred_element_type=jnp.float32)


def factor_small(block):
    lane = lax.broadcasted_iota(jnp.int32, (W, 128), 1)
    row = lax.broadcasted_iota(jnp.int32, (W, 128), 0)
    work = jnp.where(lane < W, block, 0.0)
    work = work + jnp.where((lane == row + W) | (lane == row + 2 * W), 1.0, 0.0)
    packed = work
    scale = jnp.ones((W, 128), jnp.float32)
    down = lane < 2 * W
    up = (lane < W) | (lane >= 2 * W)
    for first in range(0, W, MICRO):
        columns = [
            jnp.broadcast_to(work[:, j : j + 1], (W, 128)) for j in range(first, first + MICRO)
        ]
        for step in range(MICRO):
            j = first + step
            column = columns[step]
            inverse = 1.0 / column[j : j + 1, :]
            factor = jnp.where(row == j, 0.0, column * inverse)
            for later in range(step + 1, MICRO):
                other = columns[later]
                columns[later] = other - factor * other[j : j + 1, :]
            line = work[j : j + 1, :]
            packed = jnp.where((row == j) & (lane >= j), line, packed)
            packed = jnp.where((lane == j) & (row > j), factor, packed)
            scale = jnp.where(row == j, inverse, scale)
            masked = jnp.where(((row > j) & down) | ((row < j) & up), factor, 0.0)
            work = work - masked * line
    return jnp.where(lane < W, packed, 0.0), work, work * scale


def repeat_lanes(x, first):
    lane = lax.broadcasted_iota(jnp.int32, x.shape, 1)
    x = jnp.where((lane >= first) & (lane < first + W), x, 0.0)
    x = x + pltpu.roll(x, W, 1)
    return x + pltpu.roll(x, 2 * W, 1)


def pack_left(x):
    lane = lax.broadcasted_iota(jnp.int32, x.shape, 1)
    high = x.astype(jnp.bfloat16).astype(jnp.float32)
    rest = x - high
    middle = rest.astype(jnp.bfloat16).astype(jnp.float32)
    low = rest - middle
    first = jnp.where(lane < 3 * W, high, middle)
    second = jnp.where(lane < W, middle, jnp.where(lane < 2 * W, low, 0.0))
    return jnp.concatenate([first.astype(jnp.bfloat16), second.astype(jnp.bfloat16)], axis=1)


def pack_right(x):
    high, middle, low = split3(x)
    zero = jnp.zeros_like(high)
    return jnp.concatenate([high, middle, low, high, middle, high, zero, zero], axis=0)


def block_step(k, work_ref, lower_ref, upper_ref):
    active = NB - W * k
    packed, left_small, upper_small = factor_small(work_ref[:W, :128])
    small_left = pack_left(repeat_lanes(left_small, W))
    small_upper = repeat_lanes(upper_small, 2 * W)
    small_upper = pack_right(jnp.concatenate([small_upper, small_upper], axis=1))

    work = work_ref[...]
    lower = lower_ref[...]
    upper = upper_ref[...]
    col = lax.broadcasted_iota(jnp.int32, (W, NB), 1)
    top_old = work[:W]
    top = dot(small_left, pack_right(top_old))
    live_col = (col >= W) & (col < active)
    top_live = jnp.where(live_col, top, 0.0)
    lower_top = dot(small_left, pack_right(lower[:W]))

    row = lax.broadcasted_iota(jnp.int32, (NB, 128), 0)
    live_row = (row >= W) & (row < active)
    left_old = work[:, :128]
    left = dot(pack_left(repeat_lanes(left_old, 0)), small_upper)[:, :128]
    left_live = jnp.where(live_row, left, 0.0)
    upper_left = dot(pack_left(repeat_lanes(upper[:, :128], 0)), small_upper)[:, :128]

    left_packed = pack_left(left_live)
    top_packed = pack_right(top_live)
    work_new = work - dot(left_packed, top_packed)
    lower_new = lower - dot(left_packed, pack_right(lower_top))
    upper_new = upper - dot(pack_left(upper_left), top_packed)

    lane = lax.broadcasted_iota(jnp.int32, (NB, 128), 1)
    left_side = jnp.where((lane < W) & live_row, left, work_new[:, :128])
    work_new = jnp.concatenate([left_side, work_new[:, 128:]], axis=1)
    packed_wide = jnp.concatenate([packed, jnp.zeros_like(packed)], axis=1)
    top_new = jnp.where(col < W, packed_wide, jnp.where(live_col, top, top_old))
    work_new = jnp.concatenate([work_new[W:], top_new], axis=0)
    work_ref[...] = pltpu.roll(work_new, NB - W, 1)
    lower_ref[...] = jnp.concatenate([lower_new[W:], lower_top], axis=0)
    upper_side = jnp.where(lane < W, upper_left, upper_new[:, :128])
    upper_ref[...] = pltpu.roll(
        jnp.concatenate([upper_side, upper_new[:, 128:]], axis=1), NB - W, 1
    )


def identity():
    row = lax.broadcasted_iota(jnp.int32, (NB, NB), 0)
    col = lax.broadcasted_iota(jnp.int32, (NB, NB), 1)
    return jnp.where(row == col, 1.0, 0.0).astype(jnp.float32)


def times_right(a, b):
    high, middle, low = split3(b)
    return dot(a, high) + (dot(a, middle) + dot(a, low))


def times_left(a, b):
    high, middle, low = split3(a)
    return dot(high, b) + (dot(middle, b) + dot(low, b))


def run_steps(first, count, work_ref, lower_ref, upper_ref):
    def body(k, carry):
        block_step(k, work_ref, lower_ref, upper_ref)
        return carry

    lax.fori_loop(first, first + count, body, 0)


def pick(place_ref, blocks, i, j):
    same_row = place_ref[0] % 2 == i
    same_col = place_ref[1] % 2 == j
    own, across, below, both = [block[...].astype(jnp.float32) for block in blocks]
    near = jnp.where(same_col, own, across)
    far = jnp.where(same_col, below, both)
    return jnp.where(same_row, near, far)


def first_kernel(count, n_extra, place_ref, d0, d1, d2, d3, *refs):
    work_ref, lower_ref, upper_ref = refs[n_extra:]
    work_ref[...] = pick(place_ref, (d0, d1, d2, d3), 0, 0)
    lower_ref[...] = identity()
    upper_ref[...] = identity()
    run_steps(0, count, work_ref, lower_ref, upper_ref)


def second_kernel(count, n_extra, place_ref, d0, d1, d2, d3, inv_lower, inv_upper, *refs):
    work_ref, lower_ref, upper_ref, left_ref, top_ref = refs[n_extra:]
    blocks = (d0, d1, d2, d3)
    left = times_right(pick(place_ref, blocks, 1, 0).astype(jnp.bfloat16), inv_upper[...])
    left = left.astype(jnp.bfloat16)
    top = times_left(inv_lower[...], pick(place_ref, blocks, 0, 1).astype(jnp.bfloat16))
    top = top.astype(jnp.bfloat16)
    left_ref[...] = left
    top_ref[...] = top
    block = pick(place_ref, blocks, 1, 1) - dot(left, top)
    work_ref[...] = block.astype(jnp.bfloat16).astype(jnp.float32)
    lower_ref[...] = identity()
    upper_ref[...] = identity()
    run_steps(0, count, work_ref, lower_ref, upper_ref)


def next_kernel(first, count, n_extra, work_in, lower_in, upper_in, *refs):
    work_ref, lower_ref, upper_ref = refs[n_extra:]
    work_ref[...] = work_in[...]
    lower_ref[...] = lower_in[...]
    upper_ref[...] = upper_in[...]
    run_steps(first, count, work_ref, lower_ref, upper_ref)


def vmem():
    return pl.BlockSpec(memory_space=pltpu.VMEM)


def smem():
    return pl.BlockSpec(memory_space=pltpu.SMEM)


def anywhere():
    return pl.BlockSpec(memory_space=pl.ANY)


def factor_call(body, n_out, place, operands, extra, flops):
    square = jax.ShapeDtypeStruct((NB, NB), jnp.float32)
    panel = jax.ShapeDtypeStruct((NB, NB), jnp.bfloat16)
    scalars = [] if place is None else [place]
    return pl.pallas_call(
        body,
        out_shape=[square] * 3 + [panel] * (n_out - 3),
        in_specs=[smem() for _ in scalars] + [vmem() for _ in operands] + [anywhere() for _ in extra],
        out_specs=[vmem()] * n_out,
        compiler_params=pltpu.CompilerParams(vmem_limit_bytes=LIMIT),
        cost_estimate=pl.CostEstimate(flops=flops, bytes_accessed=2**21, transcendentals=0),
    )(*scalars, *operands, *extra)


def left_kernel(place_ref, own, other, inv_first, inv_second, top, out):
    parity = place_ref[1] % 2
    own_value = own[...].astype(jnp.float32)
    other_value = other[...].astype(jnp.float32)
    first = jnp.where(parity == 0, own_value, other_value).astype(jnp.bfloat16)
    second = jnp.where(parity == 0, other_value, own_value)
    rows = lax.broadcasted_iota(jnp.int32, (own.shape[0], NB), 0)
    outer = (rows >= NB) | (pl.program_id(0) > 0)
    left = times_right(first, inv_first[...])
    left = jnp.where(outer | (place_ref[0] > 0), left, 0.0).astype(jnp.bfloat16)
    out[:, :NB] = left
    second = (second - dot(left, top[...])).astype(jnp.bfloat16)
    left = times_right(second, inv_second[...])
    left = jnp.where(outer | (place_ref[0] > 1), left, 0.0).astype(jnp.bfloat16)
    out[:, NB:] = left


def left_call(place, own, other, inv_first, inv_second, top):
    rows = own.shape[0]
    tile = rows // 4
    whole = pl.BlockSpec((NB, NB), lambda i: (0, 0))
    return pl.pallas_call(
        left_kernel,
        grid=(4,),
        out_shape=jax.ShapeDtypeStruct((rows, 2 * NB), jnp.bfloat16),
        in_specs=[
            smem(),
            pl.BlockSpec((tile, NB), lambda i: (i, 0)),
            pl.BlockSpec((tile, NB), lambda i: (i, 0)),
            whole,
            whole,
            whole,
        ],
        out_specs=pl.BlockSpec((tile, 2 * NB), lambda i: (i, 0)),
        compiler_params=pltpu.CompilerParams(vmem_limit_bytes=LIMIT),
        cost_estimate=pl.CostEstimate(
            flops=14 * rows * NB * NB, bytes_accessed=8 * rows * NB, transcendentals=0
        ),
    )(place, own, other, inv_first, inv_second, top)


def update_kernel(first, count, lines, n_extra, place_ref, matrix, left_ref, packed_first,
                  packed_second, inv_first, inv_second, left_block, *refs):
    n_sent = count + DELAY * (lines - 1)
    own = refs[:n_sent]
    other = refs[n_sent : 2 * n_sent]
    out, raw, top_ref, sems = refs[2 * n_sent + n_extra :]
    j = pl.program_id(0)
    i = pl.program_id(1)
    grid_row = place_ref[0]
    grid_col = place_ref[1]
    line = grid_row // 2
    parity = grid_row % 2
    tile, width = out.shape

    @pl.when((i == 0) & (j == 0))
    def _():
        for c in range(count):
            for k in range(lines):
                @pl.when(line == k)
                def _():
                    s = c + DELAY * k
                    pltpu.make_async_copy(own[s], raw.at[parity, c], sems.at[0, c]).start()
                    pltpu.make_async_copy(other[s], raw.at[1 - parity, c], sems.at[1, c]).start()

    @pl.when(i == 0)
    def _():
        pltpu.make_async_copy(own[0], raw.at[parity, j], sems.at[0, j]).wait()
        pltpu.make_async_copy(other[0], raw.at[1 - parity, j], sems.at[1, j]).wait()
        cols = lax.broadcasted_iota(jnp.int32, (NB, width), 1)
        outer = (cols >= NB) | (first + j > 0)
        top = times_left(inv_first[...], raw[0, j])
        top = jnp.where(outer | (grid_col > 0), top, 0.0).astype(jnp.bfloat16)
        top_ref[:NB, :] = top
        second = raw[1, j].astype(jnp.float32) - dot(left_block[...], top)
        top = times_left(inv_second[...], second.astype(jnp.bfloat16))
        top = jnp.where(outer | (grid_col > 1), top, 0.0).astype(jnp.bfloat16)
        top_ref[NB:, :] = top

    rows = pl.ds(pl.multiple_of(i * tile, tile), tile)
    for start in range(0, width, NB):
        cols = slice(start, start + NB)
        value = matrix[:, cols].astype(jnp.float32)
        value = value - dot(left_ref[rows, :NB], top_ref[:NB, cols])
        value = value.astype(jnp.bfloat16).astype(jnp.float32)
        value = value - dot(left_ref[rows, NB:], top_ref[NB:, cols])
        out[:, cols] = value.astype(jnp.bfloat16)

    @pl.when((i == 0) & (grid_row == 0))
    def _():
        out[:NB, :] = top_ref[:NB, :]

    @pl.when((i == 0) & (grid_row == 1))
    def _():
        out[:NB, :] = top_ref[NB:, :]

    if first == 0:
        @pl.when((j == 0) & (grid_col == 0))
        def _():
            out[:, :NB] = left_ref[rows, :NB]

        @pl.when((j == 0) & (grid_col == 1))
        def _():
            out[:, :NB] = left_ref[rows, NB:]

        @pl.when((j == 0) & (i == 0) & (grid_col == 0) & (grid_row == 0))
        def _():
            out[:NB, :NB] = packed_first[...].astype(jnp.bfloat16)

        @pl.when((j == 0) & (i == 0) & (grid_col == 1) & (grid_row == 0))
        def _():
            out[:NB, :NB] = top_ref[:NB, :NB]

        @pl.when((j == 0) & (i == 0) & (grid_col == 1) & (grid_row == 1))
        def _():
            out[:NB, :NB] = packed_second[...].astype(jnp.bfloat16)


def update_call(first, last, lines, place, matrix, left, squares, left_block, own, other, extra, before):
    rows, cols = matrix.shape
    width = cols // CHUNKS
    tile = rows // 4
    count = last - first
    tail = list(extra) + ([] if before is None else [before])
    whole = pl.BlockSpec((NB, NB), lambda j, i: (0, 0))
    big = pl.BlockSpec((tile, width), lambda j, i: (i, j + first))
    operands = [place, matrix, left, *squares, left_block, *own, *other, *tail]
    aliases = {} if before is None else {len(operands) - 1: 0}
    return pl.pallas_call(
        functools.partial(update_kernel, first, count, lines, len(tail)),
        grid=(count, 4),
        out_shape=jax.ShapeDtypeStruct((rows, cols), jnp.bfloat16),
        in_specs=[smem(), big, pl.BlockSpec((rows, 2 * NB), lambda j, i: (0, 0))]
        + [whole] * 5
        + [anywhere() for _ in range(len(own) + len(other) + len(tail))],
        out_specs=big,
        scratch_shapes=[
            pltpu.VMEM((2, count, NB, width), jnp.bfloat16),
            pltpu.VMEM((2 * NB, width), jnp.bfloat16),
            pltpu.SemaphoreType.DMA((2, count)),
        ],
        input_output_aliases=aliases,
        compiler_params=pltpu.CompilerParams(vmem_limit_bytes=LIMIT),
        cost_estimate=pl.CostEstimate(
            flops=4 * rows * NB * width * count,
            bytes_accessed=4 * rows * width * count,
            transcendentals=0,
        ),
    )(*operands)


def swap(size):
    return [(i, i ^ 1) for i in range(size)]


def spread(block, axis, size, index):
    stride = size // 2
    while stride >= 2:
        pairs = [(i, i + stride) for i in range(size) if i % (2 * stride) < 2]
        moved = lax.ppermute(block, axis, pairs)
        block = jnp.where(index % (2 * stride) >= stride, moved, block)
        stride //= 2
    return block


def on_device(matrix):
    grid_rows = lax.axis_size("row")
    grid_cols = lax.axis_size("col")
    grid_row = lax.axis_index("row")
    grid_col = lax.axis_index("col")
    place = jnp.stack([grid_row, grid_col]).astype(jnp.int32)
    lines = grid_rows // 2
    width = matrix.shape[1] // CHUNKS

    diag = spread(matrix[:NB, :NB], "col", grid_cols, grid_col)
    diag = spread(diag, "row", grid_rows, grid_row)
    both_swap = [
        (i * grid_cols + j, (i ^ 1) * grid_cols + (j ^ 1))
        for i in range(grid_rows)
        for j in range(grid_cols)
    ]
    blocks = (
        diag,
        lax.ppermute(diag, "col", swap(grid_cols)),
        lax.ppermute(diag, "row", swap(grid_rows)),
        lax.ppermute(diag, ("row", "col"), both_swap),
    )

    column = spread(matrix[:, :NB], "col", grid_cols, grid_col)
    column_other = lax.ppermute(column, "col", swap(grid_cols))

    n_steps = CHUNKS + DELAY * (lines - 1)
    own, other, received = [], [], []
    for t in range(n_steps):
        if t < CHUNKS:
            send = matrix[:NB, t * width : (t + 1) * width]
            if t >= DELAY:
                send = jnp.where(grid_row < 2, send, received[t - DELAY])
        else:
            send = received[t - DELAY]
        live = [k for k in range(lines) if 0 <= t - DELAY * k < CHUNKS]
        onward = [(2 * k + e, 2 * k + 2 + e) for k in live for e in range(2) if k + 1 < lines]
        across = [(2 * k + e, 2 * k + 1 - e) for k in live for e in range(2)]
        own.append(send)
        received.append(lax.ppermute(send, "row", onward) if onward else send)
        other.append(lax.ppermute(send, "row", across))

    def ready(step):
        return own[min(step, n_steps - 1)]

    per_piece = NB // W // PIECES
    cost = 2 * 10**9
    state = factor_call(
        functools.partial(first_kernel, per_piece, 1), 3, place, blocks, [ready(FIRST_PIECE)], cost
    )
    for piece in range(1, PIECES):
        state = factor_call(
            functools.partial(next_kernel, piece * per_piece, per_piece, 1),
            3, None, state, [ready(FIRST_PIECE + piece)], cost,
        )
    packed_first, lower_first, upper_first = state
    *state, left_block, top_block = factor_call(
        functools.partial(second_kernel, per_piece, 1),
        5, place, [*blocks, lower_first, upper_first], [ready(FIRST_PIECE + PIECES)], cost,
    )
    for piece in range(1, PIECES):
        state = factor_call(
            functools.partial(next_kernel, piece * per_piece, per_piece, 1),
            3, None, state, [ready(FIRST_PIECE + PIECES + piece)], cost,
        )
    packed_second, lower_second, upper_second = state

    left = left_call(place, column, column_other, upper_first, upper_second, top_block)
    squares = (packed_first, packed_second, lower_first, lower_second)
    out = None
    for first, last in BATCHES:
        end = last + DELAY * (lines - 1)
        out = update_call(
            first, last, lines, place, matrix, left, squares, left_block,
            own[first:end], other[first:end], [ready(end)], out,
        )
    return out


def solution(mesh):
    return jax.shard_map(
        on_device, mesh=mesh, in_specs=(P("row", "col"),), out_specs=P("row", "col"), check_vma=False
    )
```

```python
import functools

import jax
import jax.numpy as jnp
from jax import lax
from jax.experimental import pallas as pl
from jax.experimental.pallas import tpu as pltpu
from jax.sharding import PartitionSpec as P

NB = 256
W = 64
MICRO = 8
CHUNKS = 7
ROW_TILES = 7
PIECES = 4
BATCHES = ((0, 2), (2, 4), (4, 6), (6, 7))
LIMIT = 56 * 2**20


def split3(x):
    high = x.astype(jnp.bfloat16)
    rest = x - high.astype(jnp.float32)
    middle = rest.astype(jnp.bfloat16)
    low = (rest - middle.astype(jnp.float32)).astype(jnp.bfloat16)
    return high, middle, low


def dot(a, b):
    return jnp.dot(a, b, preferred_element_type=jnp.float32)


def factor_small(block):
    lane = lax.broadcasted_iota(jnp.int32, (W, 128), 1)
    row = lax.broadcasted_iota(jnp.int32, (W, 128), 0)
    work = jnp.where(lane < W, block, jnp.where(lane == row + W, 1.0, 0.0))
    upper = jnp.where(lane == row, 1.0, 0.0).astype(jnp.float32)
    packed = jnp.zeros((W, 128), jnp.float32)
    scale = jnp.ones((W, 128), jnp.float32)
    for first in range(0, W, MICRO):
        columns = [
            jnp.broadcast_to(work[:, j : j + 1], (W, 128)) for j in range(first, first + MICRO)
        ]
        for step in range(MICRO):
            j = first + step
            column = columns[step]
            inverse = 1.0 / column[j : j + 1, :]
            factor = jnp.where(row == j, 0.0, column * inverse)
            for later in range(step + 1, MICRO):
                other = columns[later]
                columns[later] = other - factor * other[j : j + 1, :]
            line = work[j : j + 1, :]
            below = jnp.where(row > j, factor, 0.0)
            above = factor - below
            packed = jnp.where((row == j) & (lane >= j), line, packed)
            packed = jnp.where((lane == j) & (row > j), factor, packed)
            scale = jnp.where(row == j, inverse, scale)
            work = work - jnp.where(lane < W, factor, below) * line
            upper = upper - above * upper[j : j + 1, :]
    return packed, work, upper * scale


def repeat_lanes(x, first):
    lane = lax.broadcasted_iota(jnp.int32, x.shape, 1)
    x = jnp.where((lane >= first) & (lane < first + W), x, 0.0)
    return x + pltpu.roll(x, W, 1)


def pack_left(x):
    lane = lax.broadcasted_iota(jnp.int32, x.shape, 1)
    high = x.astype(jnp.bfloat16)
    rest = x - high.astype(jnp.float32)
    middle = rest.astype(jnp.bfloat16).astype(jnp.float32)
    low = rest - middle
    second = jnp.where(lane < W, high.astype(jnp.float32), middle).astype(jnp.bfloat16)
    third = jnp.where(lane < W, middle, low).astype(jnp.bfloat16)
    return jnp.concatenate([high, second, third], axis=1)


def pack_right(x):
    high, middle, low = split3(x)
    return jnp.concatenate([high, middle, low, high, middle, high], axis=0)


def block_step(k, work_ref, lower_ref, upper_ref):
    active = NB - W * k
    packed, left_small, upper_small = factor_small(work_ref[:W, :128])
    small_left = pack_left(repeat_lanes(left_small, W))
    small_upper = pack_right(repeat_lanes(upper_small, 0))

    work = work_ref[...]
    lower = lower_ref[...]
    upper = upper_ref[...]
    col = lax.broadcasted_iota(jnp.int32, (W, NB), 1)
    row = lax.broadcasted_iota(jnp.int32, (NB, 128), 0)
    lane = lax.broadcasted_iota(jnp.int32, (NB, 128), 1)
    live_col = (col >= W) & (col < active)
    live_row = (row >= W) & (row < active)

    tops = dot(small_left, pack_right(jnp.concatenate([work[:W], lower[:W]], axis=1)))
    top, lower_top = tops[:, :NB], tops[:, NB:]
    sides = jnp.concatenate([work[:, :128], upper[:, :128]], axis=0)
    sides = dot(pack_left(repeat_lanes(sides, 0)), small_upper)
    left, upper_left = sides[:NB], sides[NB:]
    left_live = jnp.where(live_row, left, 0.0)
    top_live = jnp.where(live_col, top, 0.0)

    right_packed = pack_right(jnp.concatenate([top_live, lower_top], axis=1))
    change = dot(pack_left(left_live), right_packed)
    upper_change = dot(pack_left(upper_left), right_packed[:, :NB])
    work_new = work - change[:, :NB]
    lower_new = lower - change[:, NB:]
    upper_new = upper - upper_change

    left_side = jnp.where((lane < W) & live_row, left, work_new[:, :128])
    work_new = jnp.concatenate([left_side, work_new[:, 128:]], axis=1)
    packed_wide = jnp.concatenate([packed, jnp.zeros_like(packed)], axis=1)
    top_new = jnp.where(col < W, packed_wide, jnp.where(live_col, top, work[:W]))
    work_new = jnp.concatenate([work_new[W:], top_new], axis=0)
    work_ref[...] = pltpu.roll(work_new, NB - W, 1)
    lower_ref[...] = jnp.concatenate([lower_new[W:], lower_top], axis=0)
    upper_side = jnp.where(lane < W, upper_left, upper_new[:, :128])
    upper_ref[...] = pltpu.roll(
        jnp.concatenate([upper_side, upper_new[:, 128:]], axis=1), NB - W, 1
    )


def identity():
    row = lax.broadcasted_iota(jnp.int32, (NB, NB), 0)
    col = lax.broadcasted_iota(jnp.int32, (NB, NB), 1)
    return jnp.where(row == col, 1.0, 0.0).astype(jnp.float32)


def split2(x):
    high = x.astype(jnp.bfloat16)
    return high, (x - high.astype(jnp.float32)).astype(jnp.bfloat16)


def times_right(a, b):
    width = b.shape[1]
    both = dot(a, jnp.concatenate(split2(b), axis=1))
    return both[:, :width] + both[:, width:]


def times_left(a, b):
    height = a.shape[0] // 2
    both = dot(a, b)
    return both[:height] + both[height:]


def run_steps(first, count, work_ref, lower_ref, upper_ref):
    def body(k, carry):
        block_step(k, work_ref, lower_ref, upper_ref)
        return carry

    lax.fori_loop(first, first + count, body, 0)


def pick(place_ref, blocks, i, j):
    same_row = place_ref[0] % 2 == i
    same_col = place_ref[1] % 2 == j
    own, across, below, both = [block[...].astype(jnp.float32) for block in blocks]
    near = jnp.where(same_col, own, across)
    far = jnp.where(same_col, below, both)
    return jnp.where(same_row, near, far)


def first_kernel(count, n_extra, place_ref, d0, d1, d2, d3, *refs):
    work_ref, lower_ref, upper_ref = refs[n_extra:][:3]
    work_ref[...] = pick(place_ref, (d0, d1, d2, d3), 0, 0)
    lower_ref[...] = identity()
    upper_ref[...] = identity()
    run_steps(0, count, work_ref, lower_ref, upper_ref)


def second_kernel(count, n_extra, place_ref, d0, d1, d2, d3, inv_lower, inv_upper, *refs):
    work_ref, lower_ref, upper_ref, left_ref, top_ref = refs[n_extra:][:5]
    blocks = (d0, d1, d2, d3)
    left = times_right(pick(place_ref, blocks, 1, 0).astype(jnp.bfloat16), inv_upper[...])
    left = left.astype(jnp.bfloat16)
    top = times_left(jnp.concatenate(split2(inv_lower[...]), axis=0), pick(place_ref, blocks, 0, 1).astype(jnp.bfloat16))
    top = top.astype(jnp.bfloat16)
    left_ref[...] = left
    top_ref[...] = top
    block = pick(place_ref, blocks, 1, 1) - dot(left, top)
    work_ref[...] = block.astype(jnp.bfloat16).astype(jnp.float32)
    lower_ref[...] = identity()
    upper_ref[...] = identity()
    run_steps(0, count, work_ref, lower_ref, upper_ref)


def next_kernel(first, count, n_extra, work_in, lower_in, upper_in, *refs):
    work_ref, lower_ref, upper_ref = refs[n_extra:][:3]
    work_ref[...] = work_in[...]
    lower_ref[...] = lower_in[...]
    upper_ref[...] = upper_in[...]
    run_steps(first, count, work_ref, lower_ref, upper_ref)


def vmem():
    return pl.BlockSpec(memory_space=pltpu.VMEM)


def smem():
    return pl.BlockSpec(memory_space=pltpu.SMEM)


def anywhere():
    return pl.BlockSpec(memory_space=pl.ANY)


def factor_call(body, n_out, place, operands, extra, flops):
    square = jax.ShapeDtypeStruct((NB, NB), jnp.float32)
    panel = jax.ShapeDtypeStruct((NB, NB), jnp.bfloat16)
    scalars = [] if place is None else [place]
    return pl.pallas_call(
        body,
        out_shape=[square] * 3 + [panel] * (n_out - 3),
        in_specs=[smem() for _ in scalars] + [vmem() for _ in operands] + [anywhere() for _ in extra],
        out_specs=[vmem()] * n_out,
        compiler_params=pltpu.CompilerParams(vmem_limit_bytes=LIMIT),
        cost_estimate=pl.CostEstimate(flops=flops, bytes_accessed=2**21, transcendentals=0),
    )(*scalars, *operands, *extra)


def gate_kernel(column, place_ref, matrix, received, *refs):
    out, sem = refs[-2:]

    @pl.when(place_ref[0] < 2)
    def _():
        pltpu.make_async_copy(matrix.at[pl.ds(0, NB), pl.ds(column, out.shape[1])], out, sem).start()

    @pl.when(place_ref[0] >= 2)
    def _():
        pltpu.make_async_copy(received, out, sem).start()

    pltpu.make_async_copy(received, out, sem).wait()


def gate_call(column, place, matrix, received, before):
    return pl.pallas_call(
        functools.partial(gate_kernel, column),
        out_shape=jax.ShapeDtypeStruct(received.shape, received.dtype),
        in_specs=[smem()] + [anywhere() for _ in range(2 + len(before))],
        out_specs=anywhere(),
        scratch_shapes=[pltpu.SemaphoreType.DMA(())],
        compiler_params=pltpu.CompilerParams(vmem_limit_bytes=LIMIT),
    )(place, matrix, received, *before)


def left_kernel(place_ref, own, other, inv_first, inv_second, top, *refs):
    out = refs[-1]
    parity = place_ref[1] % 2
    own_value = own[...].astype(jnp.float32)
    other_value = other[...].astype(jnp.float32)
    first = jnp.where(parity == 0, own_value, other_value).astype(jnp.bfloat16)
    second = jnp.where(parity == 0, other_value, own_value)
    rows = lax.broadcasted_iota(jnp.int32, (own.shape[0], NB), 0)
    outer = (rows >= NB) | (pl.program_id(0) > 0)
    left = times_right(first, inv_first[...])
    left = jnp.where(outer | (place_ref[0] > 0), left, 0.0).astype(jnp.bfloat16)
    out[:, :NB] = left
    second = (second - dot(left, top[...])).astype(jnp.bfloat16)
    left = times_right(second, inv_second[...])
    left = jnp.where(outer | (place_ref[0] > 1), left, 0.0).astype(jnp.bfloat16)
    out[:, NB:] = left


def left_call(place, own, other, inv_first, inv_second, top, extra):
    rows = own.shape[0]
    tile = rows // 4
    whole = pl.BlockSpec((NB, NB), lambda i: (0, 0))
    return pl.pallas_call(
        left_kernel,
        grid=(4,),
        out_shape=jax.ShapeDtypeStruct((rows, 2 * NB), jnp.bfloat16),
        in_specs=[
            smem(),
            pl.BlockSpec((tile, NB), lambda i: (i, 0)),
            pl.BlockSpec((tile, NB), lambda i: (i, 0)),
            whole,
            whole,
            whole,
        ]
        + [anywhere() for _ in extra],
        out_specs=pl.BlockSpec((tile, 2 * NB), lambda i: (i, 0)),
        compiler_params=pltpu.CompilerParams(vmem_limit_bytes=LIMIT),
        cost_estimate=pl.CostEstimate(
            flops=14 * rows * NB * NB, bytes_accessed=8 * rows * NB, transcendentals=0
        ),
    )(place, own, other, inv_first, inv_second, top, *extra)


def update_kernel(first, count, lines, n_extra, place_ref, matrix, left_ref, packed_first,
                  packed_second, inv_first, inv_second, left_block, *refs):
    n_sent = count + lines - 1
    own = refs[:n_sent]
    other = refs[n_sent : 2 * n_sent]
    out, raw, top_ref, inv_ref, sems = refs[2 * n_sent + n_extra :]
    j = pl.program_id(0)
    i = pl.program_id(1)
    grid_row = place_ref[0]
    grid_col = place_ref[1]
    line = grid_row // 2
    parity = grid_row % 2
    tile, width = out.shape

    @pl.when((i == 0) & (j == 0))
    def _():
        for c in range(count):
            for k in range(lines):
                @pl.when(line == k)
                def _():
                    pltpu.make_async_copy(own[c + k], raw.at[parity, c], sems.at[0, c]).start()
                    pltpu.make_async_copy(other[c + k], raw.at[1 - parity, c], sems.at[1, c]).start()
        inv_ref[0] = jnp.concatenate(split2(inv_first[...]), axis=0)
        inv_ref[1] = jnp.concatenate(split2(inv_second[...]), axis=0)

    @pl.when(i == 0)
    def _():
        pltpu.make_async_copy(own[0], raw.at[parity, j], sems.at[0, j]).wait()
        pltpu.make_async_copy(other[0], raw.at[1 - parity, j], sems.at[1, j]).wait()
        cols = lax.broadcasted_iota(jnp.int32, (NB, width), 1)
        outer = (cols >= NB) | (first + j > 0)
        top = times_left(inv_ref[0], raw[0, j])
        top = jnp.where(outer | (grid_col > 0), -top, 0.0).astype(jnp.bfloat16)
        top_ref[:NB, :] = top
        second = raw[1, j].astype(jnp.float32) + dot(left_block[...], top)
        top = times_left(inv_ref[1], second.astype(jnp.bfloat16))
        top = jnp.where(outer | (grid_col > 1), -top, 0.0).astype(jnp.bfloat16)
        top_ref[NB:, :] = top

    for start in range(0, tile, NB):
        rows = pl.ds(pl.multiple_of(i * tile + start, NB), NB)
        here = slice(start, start + NB)
        value = matrix[here, :].astype(jnp.float32) + dot(left_ref[rows, :NB], top_ref[:NB, :])
        value = value.astype(jnp.bfloat16).astype(jnp.float32)
        value = value + dot(left_ref[rows, NB:], top_ref[NB:, :])
        out[here, :] = value.astype(jnp.bfloat16)

    rows = pl.ds(pl.multiple_of(i * tile, tile), tile)

    @pl.when((i == 0) & (grid_row == 0))
    def _():
        out[:NB, :] = -top_ref[:NB, :]

    @pl.when((i == 0) & (grid_row == 1))
    def _():
        out[:NB, :] = -top_ref[NB:, :]

    if first == 0:
        @pl.when((j == 0) & (grid_col == 0))
        def _():
            out[:, :NB] = left_ref[rows, :NB]

        @pl.when((j == 0) & (grid_col == 1))
        def _():
            out[:, :NB] = left_ref[rows, NB:]

        @pl.when((j == 0) & (i == 0) & (grid_col == 0) & (grid_row == 0))
        def _():
            out[:NB, :NB] = packed_first[...].astype(jnp.bfloat16)

        @pl.when((j == 0) & (i == 0) & (grid_col == 1) & (grid_row == 0))
        def _():
            out[:NB, :NB] = -top_ref[:NB, :NB]

        @pl.when((j == 0) & (i == 0) & (grid_col == 1) & (grid_row == 1))
        def _():
            out[:NB, :NB] = packed_second[...].astype(jnp.bfloat16)


def update_call(first, last, lines, place, matrix, left, squares, left_block, own, other, extra, before):
    rows, cols = matrix.shape
    width = cols // CHUNKS
    tile = rows // ROW_TILES
    count = last - first
    tail = list(extra) + ([] if before is None else [before])
    whole = pl.BlockSpec((NB, NB), lambda j, i: (0, 0))
    big = pl.BlockSpec((tile, width), lambda j, i: (i, j + first))
    operands = [place, matrix, left, *squares, left_block, *own, *other, *tail]
    aliases = {} if before is None else {len(operands) - 1: 0}
    return pl.pallas_call(
        functools.partial(update_kernel, first, count, lines, len(tail)),
        grid=(count, ROW_TILES),
        out_shape=jax.ShapeDtypeStruct((rows, cols), jnp.bfloat16),
        in_specs=[smem(), big, pl.BlockSpec((rows, 2 * NB), lambda j, i: (0, 0))]
        + [whole] * 5
        + [anywhere() for _ in range(len(own) + len(other) + len(tail))],
        out_specs=big,
        scratch_shapes=[
            pltpu.VMEM((2, count, NB, width), jnp.bfloat16),
            pltpu.VMEM((2 * NB, width), jnp.bfloat16),
            pltpu.VMEM((2, 2 * NB, NB), jnp.bfloat16),
            pltpu.SemaphoreType.DMA((2, count)),
        ],
        input_output_aliases=aliases,
        compiler_params=pltpu.CompilerParams(vmem_limit_bytes=LIMIT),
        cost_estimate=pl.CostEstimate(
            flops=6 * rows * NB * width * count,
            bytes_accessed=6 * rows * width * count,
            transcendentals=0,
        ),
    )(*operands)


def swap(size):
    return [(i, i ^ 1) for i in range(size)]


def spread(block, axis, size, index):
    stride = size // 2
    while stride >= 2:
        pairs = [(i, i + stride) for i in range(size) if i % (2 * stride) < 2]
        moved = lax.ppermute(block, axis, pairs)
        block = jnp.where(index % (2 * stride) >= stride, moved, block)
        stride //= 2
    return block


def on_device(matrix):
    grid_rows = lax.axis_size("row")
    grid_cols = lax.axis_size("col")
    grid_row = lax.axis_index("row")
    grid_col = lax.axis_index("col")
    place = jnp.stack([grid_row, grid_col]).astype(jnp.int32)
    lines = grid_rows // 2
    width = matrix.shape[1] // CHUNKS

    diag = spread(matrix[:NB, :NB], "col", grid_cols, grid_col)
    diag = spread(diag, "row", grid_rows, grid_row)
    both_swap = [
        (i * grid_cols + j, (i ^ 1) * grid_cols + (j ^ 1))
        for i in range(grid_rows)
        for j in range(grid_cols)
    ]
    blocks = (
        diag,
        lax.ppermute(diag, "col", swap(grid_cols)),
        lax.ppermute(diag, "row", swap(grid_rows)),
        lax.ppermute(diag, ("row", "col"), both_swap),
    )

    n_ticks = CHUNKS + lines - 1
    own, other, received = [], [], []

    def move(done, late=None):
        tick = len(own)
        if tick >= n_ticks:
            return [] if tick > n_ticks else [done]
        if tick == 0:
            send = jnp.where(grid_row < 2, matrix[:NB, :width], done)
        else:
            column = min(tick, CHUNKS - 1) * width
            send = gate_call(column, place, matrix, received[-1], [other[-1], done])
        live = [k for k in range(lines) if 0 <= tick - k < CHUNKS]
        onward = [(2 * k + e, 2 * k + 2 + e) for k in live for e in range(2) if k + 1 < lines]
        across = [(2 * k + e, 2 * k + 1 - e) for k in live for e in range(2)]
        received.append(lax.ppermute(send, "row", onward) if onward else send)
        own.append(send)
        if tick == 0:
            send = gate_call(0, place, matrix, send, late)
        other.append(lax.ppermute(send, "row", across))
        return [own[tick]]

    move(diag[:1, :1], blocks[2:])
    column = spread(matrix[:, :NB], "col", grid_cols, grid_col)
    column_other = lax.ppermute(column, "col", swap(grid_cols))

    cost = 10**9
    per_piece = NB // W // PIECES
    kept = []
    for section in range(2):
        for piece in range(PIECES):
            if piece > 0:
                extra = move(square[0])
                body = functools.partial(next_kernel, piece * per_piece, per_piece, len(extra))
                square = factor_call(body, 3, None, square, extra, cost)
            elif section == 0:
                body = functools.partial(first_kernel, per_piece, 0)
                square = factor_call(body, 3, place, blocks, [], cost)
            else:
                extra = move(square[0])
                body = functools.partial(second_kernel, per_piece, len(extra))
                *square, left_block, top_block = factor_call(
                    body, 5, place, [*blocks, *kept[0][1:]], extra, cost
                )
        kept.append(square)

    packed, lower, upper = zip(*kept)
    left = left_call(place, column, column_other, *upper, top_block, move(square[0]))
    latest = left
    out = None
    for first, last in BATCHES:
        while len(own) < min(last + lines, n_ticks):
            latest = move(latest)[0]
        sent = range(first, last + lines - 1)
        out = update_call(
            first, last, lines, place, matrix, left, (*packed, *lower), left_block,
            [own[t] for t in sent], [other[t] for t in sent], [] if latest is out else [latest], out,
        )
        latest = out
    return out


def solution(mesh):
    return jax.shard_map(
        on_device, mesh=mesh, in_specs=(P("row", "col"),), out_specs=P("row", "col"), check_vma=False
    )
```

```python
import functools

import jax
import jax.numpy as jnp
from jax import lax
from jax.experimental import pallas as pl
from jax.experimental.pallas import tpu as pltpu
from jax.sharding import PartitionSpec as P

NB = 256
W = 64
MICRO = 8
CHUNKS = 7
ROW_TILES = 7
PIECES = 2
SLOTS = 4
SPLIT = 4
BATCHES = ((0, 1), (1, 2), (2, 3), (3, 4), (4, 5), (5, 6), (6, 7))
LIMIT = 56 * 2**20


def split3(x):
    high = x.astype(jnp.bfloat16)
    rest = x - high.astype(jnp.float32)
    middle = rest.astype(jnp.bfloat16)
    low = (rest - middle.astype(jnp.float32)).astype(jnp.bfloat16)
    return high, middle, low


def dot(a, b):
    return jnp.dot(a, b, preferred_element_type=jnp.float32)


def factor_small(block):
    lane = lax.broadcasted_iota(jnp.int32, (W, 128), 1)
    row = lax.broadcasted_iota(jnp.int32, (W, 128), 0)
    work = jnp.where(lane < W, block, jnp.where(lane == row + W, 1.0, 0.0))
    upper = jnp.where(lane == row, 1.0, 0.0).astype(jnp.float32)
    packed = jnp.zeros((W, 128), jnp.float32)
    scale = jnp.ones((W, 128), jnp.float32)
    for first in range(0, W, MICRO):
        columns = [
            jnp.broadcast_to(work[:, j : j + 1], (W, 128)) for j in range(first, first + MICRO)
        ]
        for step in range(MICRO):
            j = first + step
            column = columns[step]
            inverse = 1.0 / column[j : j + 1, :]
            factor = jnp.where(row == j, 0.0, column * inverse)
            for later in range(step + 1, MICRO):
                other = columns[later]
                columns[later] = other - factor * other[j : j + 1, :]
            line = work[j : j + 1, :]
            below = jnp.where(row > j, factor, 0.0)
            above = factor - below
            packed = jnp.where((row == j) & (lane >= j), line, packed)
            packed = jnp.where((lane == j) & (row > j), factor, packed)
            scale = jnp.where(row == j, inverse, scale)
            work = work - jnp.where(lane < W, factor, below) * line
            upper = upper - above * upper[j : j + 1, :]
    return packed, work, upper * scale


def repeat_lanes(x, first):
    lane = lax.broadcasted_iota(jnp.int32, x.shape, 1)
    x = jnp.where((lane >= first) & (lane < first + W), x, 0.0)
    return x + pltpu.roll(x, W, 1)


def pack_left(x):
    lane = lax.broadcasted_iota(jnp.int32, x.shape, 1)
    high = x.astype(jnp.bfloat16)
    rest = x - high.astype(jnp.float32)
    middle = rest.astype(jnp.bfloat16).astype(jnp.float32)
    low = rest - middle
    second = jnp.where(lane < W, high.astype(jnp.float32), middle).astype(jnp.bfloat16)
    third = jnp.where(lane < W, middle, low).astype(jnp.bfloat16)
    return jnp.concatenate([high, second, third], axis=1)


def pack_right(x):
    high, middle, low = split3(x)
    return jnp.concatenate([high, middle, low, high, middle, high], axis=0)


def block_step(k, work_ref, lower_ref, upper_ref):
    active = NB - W * k
    packed, left_small, upper_small = factor_small(work_ref[:W, :128])
    small_left = pack_left(repeat_lanes(left_small, W))
    small_upper = pack_right(repeat_lanes(upper_small, 0))

    work = work_ref[...]
    lower = lower_ref[...]
    upper = upper_ref[...]
    col = lax.broadcasted_iota(jnp.int32, (W, NB), 1)
    row = lax.broadcasted_iota(jnp.int32, (NB, 128), 0)
    lane = lax.broadcasted_iota(jnp.int32, (NB, 128), 1)
    live_col = (col >= W) & (col < active)
    live_row = (row >= W) & (row < active)

    tops = dot(small_left, pack_right(jnp.concatenate([work[:W], lower[:W]], axis=1)))
    top, lower_top = tops[:, :NB], tops[:, NB:]
    sides = jnp.concatenate([work[:, :128], upper[:, :128]], axis=0)
    sides = dot(pack_left(repeat_lanes(sides, 0)), small_upper)
    left, upper_left = sides[:NB], sides[NB:]
    left_live = jnp.where(live_row, left, 0.0)
    top_live = jnp.where(live_col, top, 0.0)

    right_packed = pack_right(jnp.concatenate([top_live, lower_top], axis=1))
    change = dot(pack_left(left_live), right_packed)
    upper_change = dot(pack_left(upper_left), right_packed[:, :NB])
    work_new = work - change[:, :NB]
    lower_new = lower - change[:, NB:]
    upper_new = upper - upper_change

    left_side = jnp.where((lane < W) & live_row, left, work_new[:, :128])
    work_new = jnp.concatenate([left_side, work_new[:, 128:]], axis=1)
    packed_wide = jnp.concatenate([packed, jnp.zeros_like(packed)], axis=1)
    top_new = jnp.where(col < W, packed_wide, jnp.where(live_col, top, work[:W]))
    work_new = jnp.concatenate([work_new[W:], top_new], axis=0)
    work_ref[...] = pltpu.roll(work_new, NB - W, 1)
    lower_ref[...] = jnp.concatenate([lower_new[W:], lower_top], axis=0)
    upper_side = jnp.where(lane < W, upper_left, upper_new[:, :128])
    upper_ref[...] = pltpu.roll(
        jnp.concatenate([upper_side, upper_new[:, 128:]], axis=1), NB - W, 1
    )


def identity():
    row = lax.broadcasted_iota(jnp.int32, (NB, NB), 0)
    col = lax.broadcasted_iota(jnp.int32, (NB, NB), 1)
    return jnp.where(row == col, 1.0, 0.0).astype(jnp.float32)


def split2(x):
    high = x.astype(jnp.bfloat16)
    return high, (x - high.astype(jnp.float32)).astype(jnp.bfloat16)


def times_right(a, b):
    width = b.shape[1]
    both = dot(a, jnp.concatenate(split2(b), axis=1))
    return both[:, :width] + both[:, width:]


def times_left(a, b):
    height = a.shape[0] // 2
    both = dot(a, b)
    return both[:height] + both[height:]


def run_steps(first, count, work_ref, lower_ref, upper_ref):
    def body(k, carry):
        block_step(k, work_ref, lower_ref, upper_ref)
        return carry

    lax.fori_loop(first, first + count, body, 0)


def pick(place_ref, blocks, i, j):
    same_row = place_ref[0] % 2 == i
    same_col = place_ref[1] % 2 == j
    own, across, below, both = [block[...].astype(jnp.float32) for block in blocks]
    near = jnp.where(same_col, own, across)
    far = jnp.where(same_col, below, both)
    return jnp.where(same_row, near, far)


def first_kernel(count, n_extra, place_ref, d0, d1, d2, d3, *refs):
    work_ref, lower_ref, upper_ref = refs[n_extra:][:3]
    work_ref[...] = pick(place_ref, (d0, d1, d2, d3), 0, 0)
    lower_ref[...] = identity()
    upper_ref[...] = identity()
    run_steps(0, count, work_ref, lower_ref, upper_ref)


def second_kernel(count, n_extra, place_ref, d0, d1, d2, d3, inv_lower, inv_upper, *refs):
    work_ref, lower_ref, upper_ref, left_ref, top_ref = refs[n_extra:][:5]
    blocks = (d0, d1, d2, d3)
    left = times_right(pick(place_ref, blocks, 1, 0).astype(jnp.bfloat16), inv_upper[...])
    left = left.astype(jnp.bfloat16)
    top = times_left(jnp.concatenate(split2(inv_lower[...]), axis=0), pick(place_ref, blocks, 0, 1).astype(jnp.bfloat16))
    top = top.astype(jnp.bfloat16)
    left_ref[...] = left
    top_ref[...] = top
    block = pick(place_ref, blocks, 1, 1) - dot(left, top)
    work_ref[...] = block.astype(jnp.bfloat16).astype(jnp.float32)
    lower_ref[...] = identity()
    upper_ref[...] = identity()
    run_steps(0, count, work_ref, lower_ref, upper_ref)


def next_kernel(first, count, n_extra, work_in, lower_in, upper_in, *refs):
    work_ref, lower_ref, upper_ref = refs[n_extra:][:3]
    work_ref[...] = work_in[...]
    lower_ref[...] = lower_in[...]
    upper_ref[...] = upper_in[...]
    run_steps(first, count, work_ref, lower_ref, upper_ref)


def vmem():
    return pl.BlockSpec(memory_space=pltpu.VMEM)


def smem():
    return pl.BlockSpec(memory_space=pltpu.SMEM)


def anywhere():
    return pl.BlockSpec(memory_space=pl.ANY)


def factor_call(body, n_out, place, operands, extra, flops):
    square = jax.ShapeDtypeStruct((NB, NB), jnp.float32)
    panel = jax.ShapeDtypeStruct((NB, NB), jnp.bfloat16)
    scalars = [] if place is None else [place]
    return pl.pallas_call(
        body,
        out_shape=[square] * 3 + [panel] * (n_out - 3),
        in_specs=[smem() for _ in scalars] + [vmem() for _ in operands] + [anywhere() for _ in extra],
        out_specs=[vmem()] * n_out,
        compiler_params=pltpu.CompilerParams(vmem_limit_bytes=LIMIT),
        cost_estimate=pl.CostEstimate(flops=flops, bytes_accessed=2**21, transcendentals=0),
    )(*scalars, *operands, *extra)


def gate_kernel(column, place_ref, received, matrix, *refs):
    out, sem = refs[-2:]

    @pl.when(place_ref[0] < 2)
    def _():
        copy = pltpu.make_async_copy(
            matrix.at[pl.ds(0, NB), pl.ds(column, out.shape[1])], out, sem
        )
        copy.start()
        copy.wait()

    @pl.when(place_ref[0] >= 2)
    def _():
        out[...] = received[...]


def gate_call(column, place, matrix, received, before):
    return pl.pallas_call(
        functools.partial(gate_kernel, column),
        out_shape=jax.ShapeDtypeStruct(received.shape, received.dtype),
        in_specs=[smem(), vmem()] + [anywhere() for _ in range(1 + len(before))],
        out_specs=vmem(),
        scratch_shapes=[pltpu.SemaphoreType.DMA(())],
        compiler_params=pltpu.CompilerParams(vmem_limit_bytes=LIMIT),
    )(place, received, matrix, *before)


def hold_kernel(*refs):
    pass


def hold_call(value, before):
    return pl.pallas_call(
        hold_kernel,
        out_shape=jax.ShapeDtypeStruct(value.shape, value.dtype),
        in_specs=[anywhere() for _ in range(1 + len(before))],
        out_specs=anywhere(),
        input_output_aliases={0: 0},
        compiler_params=pltpu.CompilerParams(vmem_limit_bytes=LIMIT),
    )(value, *before)


def left_kernel(place_ref, own, other, inv_first, inv_second, top, *refs):
    out = refs[-1]
    parity = place_ref[1] % 2
    own_value = own[...].astype(jnp.float32)
    other_value = other[...].astype(jnp.float32)
    first = jnp.where(parity == 0, own_value, other_value).astype(jnp.bfloat16)
    second = jnp.where(parity == 0, other_value, own_value)
    rows = lax.broadcasted_iota(jnp.int32, (own.shape[0], NB), 0)
    outer = (rows >= NB) | (pl.program_id(0) > 0)
    left = times_right(first, inv_first[...])
    left = jnp.where(outer | (place_ref[0] > 0), left, 0.0).astype(jnp.bfloat16)
    out[:, :NB] = left
    second = (second - dot(left, top[...])).astype(jnp.bfloat16)
    left = times_right(second, inv_second[...])
    left = jnp.where(outer | (place_ref[0] > 1), left, 0.0).astype(jnp.bfloat16)
    out[:, NB:] = left


def left_call(place, own, other, inv_first, inv_second, top, extra):
    rows = own.shape[0]
    tile = rows // 4
    whole = pl.BlockSpec((NB, NB), lambda i: (0, 0))
    return pl.pallas_call(
        left_kernel,
        grid=(4,),
        out_shape=jax.ShapeDtypeStruct((rows, 2 * NB), jnp.bfloat16),
        in_specs=[
            smem(),
            pl.BlockSpec((tile, NB), lambda i: (i, 0)),
            pl.BlockSpec((tile, NB), lambda i: (i, 0)),
            whole,
            whole,
            whole,
        ]
        + [anywhere() for _ in extra],
        out_specs=pl.BlockSpec((tile, 2 * NB), lambda i: (i, 0)),
        compiler_params=pltpu.CompilerParams(vmem_limit_bytes=LIMIT),
        cost_estimate=pl.CostEstimate(
            flops=14 * rows * NB * NB, bytes_accessed=8 * rows * NB, transcendentals=0
        ),
    )(place, own, other, inv_first, inv_second, top, *extra)


def update_kernel(first, count, lines, n_extra, place_ref, left_ref, packed_first, packed_second,
                  inv_first, inv_second, left_block, matrix, *refs):
    n_sent = count + lines - 1
    own = refs[:n_sent]
    other = refs[n_sent : 2 * n_sent]
    out, raw, top_ref, inv_ref, reads, writes, raw_sems, read_sems, write_sems = refs[2 * n_sent + n_extra :]
    grid_row = place_ref[0]
    grid_col = place_ref[1]
    line = grid_row // 2
    parity = grid_row % 2
    tile, width = reads.shape[1:]
    steps = count * ROW_TILES
    part = tile // SPLIT

    def window(step, begin, size):
        top = pl.multiple_of(step % ROW_TILES * tile + begin, 16)
        side = pl.multiple_of((first + step // ROW_TILES) * width, 128)
        return pl.ds(top, size), pl.ds(side, width)

    def read(step):
        slot = step % SLOTS
        for n in range(SPLIT):
            pltpu.make_async_copy(
                matrix.at[window(step, n * part, part)],
                reads.at[slot, pl.ds(n * part, part)],
                read_sems.at[slot],
            ).start()

    def wait_read(step):
        slot = step % SLOTS
        pltpu.make_async_copy(matrix.at[window(step, 0, tile)], reads.at[slot], read_sems.at[slot]).wait()

    def write(step):
        slot = step % SLOTS
        for n in range(SPLIT):
            pltpu.make_async_copy(
                writes.at[slot, pl.ds(n * part, part)],
                out.at[window(step, n * part, part)],
                write_sems.at[slot],
            ).start()

    def wait_write(step):
        slot = step % SLOTS
        pltpu.make_async_copy(writes.at[slot], out.at[window(step, 0, tile)], write_sems.at[slot]).wait()

    for c in range(count):
        for k in range(lines):
            @pl.when(line == k)
            def _():
                pltpu.make_async_copy(own[c + k], raw.at[parity, c], raw_sems.at[0, c]).start()
                pltpu.make_async_copy(other[c + k], raw.at[1 - parity, c], raw_sems.at[1, c]).start()
    for step in range(SLOTS - 1):
        read(step)
    inv_ref[0] = jnp.concatenate(split2(inv_first[...]), axis=0)
    inv_ref[1] = jnp.concatenate(split2(inv_second[...]), axis=0)

    def solve_top(j):
        pltpu.make_async_copy(own[0], raw.at[parity, j], raw_sems.at[0, j]).wait()
        pltpu.make_async_copy(other[0], raw.at[1 - parity, j], raw_sems.at[1, j]).wait()
        cols = lax.broadcasted_iota(jnp.int32, (NB, width), 1)
        outer = (cols >= NB) | (first + j > 0)
        top = times_left(inv_ref[0], raw[0, j])
        top = jnp.where(outer | (grid_col > 0), -top, 0.0).astype(jnp.bfloat16)
        top_ref[:NB, :] = top
        second = raw[1, j].astype(jnp.float32) + dot(left_block[...], top)
        top = times_left(inv_ref[1], second.astype(jnp.bfloat16))
        top = jnp.where(outer | (grid_col > 1), -top, 0.0).astype(jnp.bfloat16)
        top_ref[NB:, :] = top

    def body(step, carry):
        i = step % ROW_TILES
        j = step // ROW_TILES
        slot = step % SLOTS

        @pl.when(step + SLOTS - 1 < steps)
        def _():
            read(step + SLOTS - 1)

        @pl.when(i == 0)
        def _():
            solve_top(j)

        wait_read(step)

        @pl.when(step >= SLOTS)
        def _():
            wait_write(step - SLOTS)

        rows = pl.ds(pl.multiple_of(i * tile, NB), tile)
        left = left_ref[rows, :]

        def products(start):
            cols = slice(start, min(start + NB, width))
            return dot(left[:, :NB], top_ref[:NB, cols]), dot(left[:, NB:], top_ref[NB:, cols])

        ahead = products(0)
        for start in range(0, width, NB):
            cols = slice(start, min(start + NB, width))
            first_change, second_change = ahead
            if start + NB < width:
                ahead = products(start + NB)
            value = reads[slot, :, cols].astype(jnp.float32) + first_change
            value = value.astype(jnp.bfloat16).astype(jnp.float32) + second_change
            writes[slot, :, cols] = value.astype(jnp.bfloat16)

        @pl.when((i == 0) & (grid_row == 0))
        def _():
            writes[slot, :NB, :] = -top_ref[:NB, :]

        @pl.when((i == 0) & (grid_row == 1))
        def _():
            writes[slot, :NB, :] = -top_ref[NB:, :]

        if first == 0:
            @pl.when((j == 0) & (grid_col == 0))
            def _():
                writes[slot, :, :NB] = left_ref[rows, :NB]

            @pl.when((j == 0) & (grid_col == 1))
            def _():
                writes[slot, :, :NB] = left_ref[rows, NB:]

            @pl.when((j == 0) & (i == 0) & (grid_col == 0) & (grid_row == 0))
            def _():
                writes[slot, :NB, :NB] = packed_first[...].astype(jnp.bfloat16)

            @pl.when((j == 0) & (i == 0) & (grid_col == 1) & (grid_row == 0))
            def _():
                writes[slot, :NB, :NB] = -top_ref[:NB, :NB]

            @pl.when((j == 0) & (i == 0) & (grid_col == 1) & (grid_row == 1))
            def _():
                writes[slot, :NB, :NB] = packed_second[...].astype(jnp.bfloat16)

        write(step)
        return carry

    lax.fori_loop(0, steps, body, 0)
    for step in range(steps - SLOTS, steps):
        wait_write(step)


def update_call(first, last, lines, place, matrix, left, squares, left_block, own, other, extra, before):
    rows, cols = matrix.shape
    width = cols // CHUNKS
    tile = rows // ROW_TILES
    count = last - first
    tail = list(extra) + ([] if before is None else [before])
    operands = [place, left, *squares, left_block, matrix, *own, *other, *tail]
    aliases = {} if before is None else {len(operands) - 1: 0}
    return pl.pallas_call(
        functools.partial(update_kernel, first, count, lines, len(tail)),
        out_shape=jax.ShapeDtypeStruct((rows, cols), jnp.bfloat16),
        in_specs=[smem()]
        + [vmem()] * 6
        + [anywhere() for _ in range(1 + len(own) + len(other) + len(tail))],
        out_specs=anywhere(),
        scratch_shapes=[
            pltpu.VMEM((2, count, NB, width), jnp.bfloat16),
            pltpu.VMEM((2 * NB, width), jnp.bfloat16),
            pltpu.VMEM((2, 2 * NB, NB), jnp.bfloat16),
            pltpu.VMEM((SLOTS, tile, width), jnp.bfloat16),
            pltpu.VMEM((SLOTS, tile, width), jnp.bfloat16),
            pltpu.SemaphoreType.DMA((2, count)),
            pltpu.SemaphoreType.DMA((SLOTS,)),
            pltpu.SemaphoreType.DMA((SLOTS,)),
        ],
        input_output_aliases=aliases,
        compiler_params=pltpu.CompilerParams(vmem_limit_bytes=LIMIT),
        cost_estimate=pl.CostEstimate(
            flops=6 * rows * NB * width * count,
            bytes_accessed=6 * rows * width * count,
            transcendentals=0,
        ),
    )(*operands)


def swap(size):
    return [(i, i ^ 1) for i in range(size)]


def spread(block, axis, reach, index, size):
    stride = reach // 2
    while stride >= 2:
        pairs = [(i, i + stride) for i in range(size) if i % (2 * stride) < 2]
        moved = lax.ppermute(block, axis, pairs)
        block = jnp.where(index % (2 * stride) >= stride, moved, block)
        stride //= 2
    return block


def on_device(matrix):
    grid_rows = lax.axis_size("row")
    grid_cols = lax.axis_size("col")
    grid_row = lax.axis_index("row")
    grid_col = lax.axis_index("col")
    place = jnp.stack([grid_row, grid_col]).astype(jnp.int32)
    lines = grid_rows // 2
    width = matrix.shape[1] // CHUNKS

    diag = spread(matrix[:NB, :NB], "col", grid_cols, grid_col, grid_cols)
    diag = spread(diag, "row", grid_rows, grid_row, grid_rows)
    both_swap = [
        (i * grid_cols + j, (i ^ 1) * grid_cols + (j ^ 1))
        for i in range(grid_rows)
        for j in range(grid_cols)
    ]
    blocks = (
        diag,
        lax.ppermute(diag, "col", swap(grid_cols)),
        lax.ppermute(diag, "row", swap(grid_rows)),
        lax.ppermute(diag, ("row", "col"), both_swap),
    )

    n_ticks = CHUNKS + lines - 1
    own, other, received = [], [], []

    def move(done):
        tick = len(own)
        if tick >= n_ticks:
            return done[:1]
        if tick == 0:
            send = jnp.where(grid_row < 2, matrix[:NB, :width], diag[:1, :1])
        else:
            column = min(tick, CHUNKS - 1) * width
            send = gate_call(column, place, matrix, received[-1], [*other[-2:-1], *done])
        live = [k for k in range(lines) if 0 <= tick - k < CHUNKS]
        onward = [(2 * k + e, 2 * k + 2 + e) for k in live for e in range(2) if k + 1 < lines]
        across = [(2 * k + e, 2 * k + 1 - e) for k in live for e in range(2)]
        received.append(lax.ppermute(send, "row", onward) if onward else send)
        own.append(send)
        if tick == 0:
            send = gate_call(0, place, matrix, send, done)
        other.append(lax.ppermute(send, "row", across))
        return [send]

    move(blocks[2:])
    extra = []
    stride = grid_cols // 2
    column = matrix[:, :NB]
    pairs = [(i, i + stride) for i in range(grid_cols) if i % (2 * stride) < 2]
    moved = lax.ppermute(column, "col", pairs)

    cost = 10**9
    per_piece = NB // W // PIECES
    kept = []
    for section in range(2):
        for piece in range(PIECES):
            if section + piece > 0:
                extra = move(square[:1])
            if section > 0 and piece == 0:
                moved = hold_call(moved, extra)
                extra = [*extra, moved]
            if piece > 0:
                body = functools.partial(next_kernel, piece * per_piece, per_piece, len(extra))
                square = factor_call(body, 3, None, square, extra, cost)
            elif section == 0:
                body = functools.partial(first_kernel, per_piece, len(extra))
                square = factor_call(body, 3, place, blocks, extra, cost)
            else:
                body = functools.partial(second_kernel, per_piece, len(extra))
                *square, left_block, top_block = factor_call(
                    body, 5, place, [*blocks, *kept[0][1:]], extra, cost
                )
        kept.append(square)

    packed, lower, upper = zip(*kept)
    column = jnp.where(grid_col % (2 * stride) >= stride, moved, column)
    column = spread(column, "col", stride, grid_col, grid_cols)
    column_other = lax.ppermute(column, "col", swap(grid_cols))
    left = left_call(place, column, column_other, *upper, top_block, move(square[:1]))
    latest = left
    out = None
    for first, last in BATCHES:
        while len(own) < min(last + lines, n_ticks):
            latest = move([latest])[0]
        sent = range(first, last + lines - 1)
        out = update_call(
            first, last, lines, place, matrix, left, (*packed, *lower), left_block,
            [own[t] for t in sent], [other[t] for t in sent], [] if latest is out else [latest], out,
        )
        latest = out
    return out


def solution(mesh):
    return jax.shard_map(
        on_device, mesh=mesh, in_specs=(P("row", "col"),), out_specs=P("row", "col"), check_vma=False
    )
```

```python
import functools

import jax
import jax.numpy as jnp
from jax import lax
from jax.experimental import pallas as pl
from jax.experimental.pallas import tpu as pltpu
from jax.sharding import PartitionSpec as P

NB = 256
W = 64
MICRO = 8
CHUNKS = 7
ROW_TILES = 7
PIECES = 2
SLOTS = 4
SPLIT = 4
BATCHES = ((0, 1), (1, 2), (2, 3), (3, 4), (4, 5), (5, 6), (6, 7))
MIB = 2**20


def split3(x):
    high = x.astype(jnp.bfloat16)
    rest = x - high.astype(jnp.float32)
    middle = rest.astype(jnp.bfloat16)
    low = (rest - middle.astype(jnp.float32)).astype(jnp.bfloat16)
    return high, middle, low


def dot(a, b):
    return jnp.dot(a, b, preferred_element_type=jnp.float32)


def factor_small(block):
    lane = lax.broadcasted_iota(jnp.int32, (W, 128), 1)
    row = lax.broadcasted_iota(jnp.int32, (W, 128), 0)
    work = jnp.where(lane < W, block, jnp.where(lane == row + W, 1.0, 0.0))
    upper = jnp.where(lane == row, 1.0, 0.0).astype(jnp.float32)
    packed = jnp.zeros((W, 128), jnp.float32)
    scale = jnp.ones((W, 128), jnp.float32)
    for first in range(0, W, MICRO):
        columns = [
            jnp.broadcast_to(work[:, j : j + 1], (W, 128)) for j in range(first, first + MICRO)
        ]
        for step in range(MICRO):
            j = first + step
            column = columns[step]
            inverse = 1.0 / column[j : j + 1, :]
            factor = jnp.where(row == j, 0.0, column * inverse)
            for later in range(step + 1, MICRO):
                other = columns[later]
                columns[later] = other - factor * other[j : j + 1, :]
            line = work[j : j + 1, :]
            below = jnp.where(row > j, factor, 0.0)
            above = factor - below
            packed = jnp.where((row == j) & (lane >= j), line, packed)
            packed = jnp.where((lane == j) & (row > j), factor, packed)
            scale = jnp.where(row == j, inverse, scale)
            work = work - jnp.where(lane < W, factor, below) * line
            upper = upper - above * upper[j : j + 1, :]
    return packed, work, upper * scale


def repeat_lanes(x, first):
    lane = lax.broadcasted_iota(jnp.int32, x.shape, 1)
    x = jnp.where((lane >= first) & (lane < first + W), x, 0.0)
    return x + pltpu.roll(x, W, 1)


def pack_left(x):
    lane = lax.broadcasted_iota(jnp.int32, x.shape, 1)
    high = x.astype(jnp.bfloat16)
    rest = x - high.astype(jnp.float32)
    middle = rest.astype(jnp.bfloat16).astype(jnp.float32)
    low = rest - middle
    second = jnp.where(lane < W, high.astype(jnp.float32), middle).astype(jnp.bfloat16)
    third = jnp.where(lane < W, middle, low).astype(jnp.bfloat16)
    return jnp.concatenate([high, second, third], axis=1)


def pack_right(x):
    high, middle, low = split3(x)
    return jnp.concatenate([high, middle, low, high, middle, high], axis=0)


def block_step(k, work_ref, lower_ref, upper_ref):
    active = NB - W * k
    packed, left_small, upper_small = factor_small(work_ref[:W, :128])
    small_left = pack_left(repeat_lanes(left_small, W))
    small_upper = pack_right(repeat_lanes(upper_small, 0))

    work = work_ref[...]
    lower = lower_ref[...]
    upper = upper_ref[...]
    col = lax.broadcasted_iota(jnp.int32, (W, NB), 1)
    row = lax.broadcasted_iota(jnp.int32, (NB, 128), 0)
    lane = lax.broadcasted_iota(jnp.int32, (NB, 128), 1)
    live_col = (col >= W) & (col < active)
    live_row = (row >= W) & (row < active)

    tops = dot(small_left, pack_right(jnp.concatenate([work[:W], lower[:W]], axis=1)))
    top, lower_top = tops[:, :NB], tops[:, NB:]
    sides = jnp.concatenate([work[:, :128], upper[:, :128]], axis=0)
    sides = dot(pack_left(repeat_lanes(sides, 0)), small_upper)
    left, upper_left = sides[:NB], sides[NB:]
    left_live = jnp.where(live_row, left, 0.0)
    top_live = jnp.where(live_col, top, 0.0)

    right_packed = pack_right(jnp.concatenate([top_live, lower_top], axis=1))
    change = dot(pack_left(left_live), right_packed)
    upper_change = dot(pack_left(upper_left), right_packed[:, :NB])
    work_new = work - change[:, :NB]
    lower_new = lower - change[:, NB:]
    upper_new = upper - upper_change

    left_side = jnp.where((lane < W) & live_row, left, work_new[:, :128])
    work_new = jnp.concatenate([left_side, work_new[:, 128:]], axis=1)
    packed_wide = jnp.concatenate([packed, jnp.zeros_like(packed)], axis=1)
    top_new = jnp.where(col < W, packed_wide, jnp.where(live_col, top, work[:W]))
    work_new = jnp.concatenate([work_new[W:], top_new], axis=0)
    work_ref[...] = pltpu.roll(work_new, NB - W, 1)
    lower_ref[...] = jnp.concatenate([lower_new[W:], lower_top], axis=0)
    upper_side = jnp.where(lane < W, upper_left, upper_new[:, :128])
    upper_ref[...] = pltpu.roll(
        jnp.concatenate([upper_side, upper_new[:, 128:]], axis=1), NB - W, 1
    )


def identity():
    row = lax.broadcasted_iota(jnp.int32, (NB, NB), 0)
    col = lax.broadcasted_iota(jnp.int32, (NB, NB), 1)
    return jnp.where(row == col, 1.0, 0.0).astype(jnp.float32)


def split2(x):
    high = x.astype(jnp.bfloat16)
    return high, (x - high.astype(jnp.float32)).astype(jnp.bfloat16)


def times_right(a, b):
    return dot(jnp.concatenate([a, a], axis=1), jnp.concatenate(split2(b), axis=0))


def times_left(a, b):
    return dot(a, jnp.concatenate([b, b], axis=0))


def run_steps(first, count, work_ref, lower_ref, upper_ref):
    def body(k, carry):
        block_step(k, work_ref, lower_ref, upper_ref)
        return carry

    lax.fori_loop(first, first + count, body, 0)


def pick(place_ref, blocks, i, j):
    same_row = place_ref[0] % 2 == i
    same_col = place_ref[1] % 2 == j
    own, across, below, both = [block[...].astype(jnp.float32) for block in blocks]
    near = jnp.where(same_col, own, across)
    far = jnp.where(same_col, below, both)
    return jnp.where(same_row, near, far)


def first_kernel(count, n_extra, place_ref, d0, d1, d2, d3, *refs):
    work_ref, lower_ref, upper_ref = refs[n_extra:][:3]
    work_ref[...] = pick(place_ref, (d0, d1, d2, d3), 0, 0)
    lower_ref[...] = identity()
    upper_ref[...] = identity()
    run_steps(0, count, work_ref, lower_ref, upper_ref)


def second_kernel(count, n_extra, place_ref, d0, d1, d2, d3, inv_lower, inv_upper, *refs):
    work_ref, lower_ref, upper_ref, left_ref, top_ref = refs[n_extra:][:5]
    blocks = (d0, d1, d2, d3)
    left = times_right(pick(place_ref, blocks, 1, 0).astype(jnp.bfloat16), inv_upper[...])
    left = left.astype(jnp.bfloat16)
    top = times_left(jnp.concatenate(split2(inv_lower[...]), axis=1), pick(place_ref, blocks, 0, 1).astype(jnp.bfloat16))
    top = top.astype(jnp.bfloat16)
    left_ref[...] = left
    top_ref[...] = top
    block = pick(place_ref, blocks, 1, 1) - dot(left, top)
    work_ref[...] = block.astype(jnp.bfloat16).astype(jnp.float32)
    lower_ref[...] = identity()
    upper_ref[...] = identity()
    run_steps(0, count, work_ref, lower_ref, upper_ref)


def next_kernel(first, count, n_extra, work_in, lower_in, upper_in, *refs):
    work_ref, lower_ref, upper_ref = refs[n_extra:][:3]
    work_ref[...] = work_in[...]
    lower_ref[...] = lower_in[...]
    upper_ref[...] = upper_in[...]
    run_steps(first, count, work_ref, lower_ref, upper_ref)


def vmem():
    return pl.BlockSpec(memory_space=pltpu.VMEM)


def smem():
    return pl.BlockSpec(memory_space=pltpu.SMEM)


def hbm():
    return pl.BlockSpec(memory_space=pltpu.HBM)


def anywhere():
    return pl.BlockSpec(memory_space=pl.ANY)


def factor_call(body, n_out, place, operands, extra, flops):
    square = jax.ShapeDtypeStruct((NB, NB), jnp.float32)
    panel = jax.ShapeDtypeStruct((NB, NB), jnp.bfloat16)
    scalars = [] if place is None else [place]
    return pl.pallas_call(
        body,
        out_shape=[square] * 3 + [panel] * (n_out - 3),
        in_specs=[smem() for _ in scalars] + [vmem() for _ in operands] + [anywhere() for _ in extra],
        out_specs=[vmem()] * n_out,
        compiler_params=pltpu.CompilerParams(vmem_limit_bytes=10 * MIB),
        cost_estimate=pl.CostEstimate(flops=flops, bytes_accessed=2**21, transcendentals=0),
    )(*scalars, *operands, *extra)


def gate_kernel(column, place_ref, received, matrix, *refs):
    out, sem = refs[-2:]

    @pl.when(place_ref[0] < 2)
    def _():
        copy = pltpu.make_async_copy(
            matrix.at[pl.ds(0, NB), pl.ds(column, out.shape[1])], out, sem
        )
        copy.start()
        copy.wait()

    @pl.when(place_ref[0] >= 2)
    def _():
        out[...] = received[...]


def gate_call(column, place, matrix, received, before):
    return pl.pallas_call(
        functools.partial(gate_kernel, column),
        out_shape=jax.ShapeDtypeStruct(received.shape, received.dtype),
        in_specs=[smem(), vmem(), hbm()] + [anywhere() for _ in before],
        out_specs=vmem(),
        scratch_shapes=[pltpu.SemaphoreType.DMA(())],
        compiler_params=pltpu.CompilerParams(vmem_limit_bytes=24 * MIB),
    )(place, received, matrix, *before)


def hold_kernel(*refs):
    pass


def hold_call(value, before):
    return pl.pallas_call(
        hold_kernel,
        out_shape=jax.ShapeDtypeStruct(value.shape, value.dtype),
        in_specs=[anywhere() for _ in range(1 + len(before))],
        out_specs=anywhere(),
        input_output_aliases={0: 0},
        compiler_params=pltpu.CompilerParams(vmem_limit_bytes=MIB),
    )(value, *before)


def left_kernel(place_ref, own, other, inv_first, inv_second, top, *refs):
    out = refs[-1]
    parity = place_ref[1] % 2
    own_value = own[...].astype(jnp.float32)
    other_value = other[...].astype(jnp.float32)
    first = jnp.where(parity == 0, own_value, other_value).astype(jnp.bfloat16)
    second = jnp.where(parity == 0, other_value, own_value)
    rows = lax.broadcasted_iota(jnp.int32, (own.shape[0], NB), 0)
    outer = (rows >= NB) | (pl.program_id(0) > 0)
    left = times_right(first, inv_first[...])
    left = jnp.where(outer | (place_ref[0] > 0), left, 0.0).astype(jnp.bfloat16)
    out[:, :NB] = left
    second = (second - dot(left, top[...])).astype(jnp.bfloat16)
    left = times_right(second, inv_second[...])
    left = jnp.where(outer | (place_ref[0] > 1), left, 0.0).astype(jnp.bfloat16)
    out[:, NB:] = left


def left_call(place, own, other, inv_first, inv_second, top, extra):
    rows = own.shape[0]
    tile = rows // 4
    whole = pl.BlockSpec((NB, NB), lambda i: (0, 0))
    return pl.pallas_call(
        left_kernel,
        grid=(4,),
        out_shape=jax.ShapeDtypeStruct((rows, 2 * NB), jnp.bfloat16),
        in_specs=[
            smem(),
            pl.BlockSpec((tile, NB), lambda i: (i, 0)),
            pl.BlockSpec((tile, NB), lambda i: (i, 0)),
            whole,
            whole,
            whole,
        ]
        + [anywhere() for _ in extra],
        out_specs=pl.BlockSpec((tile, 2 * NB), lambda i: (i, 0)),
        compiler_params=pltpu.CompilerParams(vmem_limit_bytes=12 * MIB),
        cost_estimate=pl.CostEstimate(
            flops=14 * rows * NB * NB, bytes_accessed=8 * rows * NB, transcendentals=0
        ),
    )(place, own, other, inv_first, inv_second, top, *extra)


def update_kernel(first, count, lines, n_extra, place_ref, left_ref, packed_first, packed_second,
                  inv_first, inv_second, left_block, matrix, *refs):
    n_sent = count + lines - 1
    own = refs[:n_sent]
    other = refs[n_sent : 2 * n_sent]
    out, raw, top_ref, inv_ref, reads, writes, raw_sems, read_sems, write_sems = refs[2 * n_sent + n_extra :]
    grid_row = place_ref[0]
    grid_col = place_ref[1]
    line = grid_row // 2
    parity = grid_row % 2
    tile, width = reads.shape[1:]
    steps = count * ROW_TILES
    part = tile // SPLIT

    def window(step, begin, size):
        top = pl.multiple_of(step % ROW_TILES * tile + begin, 16)
        side = pl.multiple_of((first + step // ROW_TILES) * width, 128)
        return pl.ds(top, size), pl.ds(side, width)

    def read(step):
        slot = step % SLOTS
        for n in range(SPLIT):
            pltpu.make_async_copy(
                matrix.at[window(step, n * part, part)],
                reads.at[slot, pl.ds(n * part, part)],
                read_sems.at[slot],
            ).start()

    def wait_read(step):
        slot = step % SLOTS
        pltpu.make_async_copy(matrix.at[window(step, 0, tile)], reads.at[slot], read_sems.at[slot]).wait()

    def write(step):
        slot = step % SLOTS
        for n in range(SPLIT):
            pltpu.make_async_copy(
                writes.at[slot, pl.ds(n * part, part)],
                out.at[window(step, n * part, part)],
                write_sems.at[slot],
            ).start()

    def wait_write(step):
        slot = step % SLOTS
        pltpu.make_async_copy(writes.at[slot], out.at[window(step, 0, tile)], write_sems.at[slot]).wait()

    for c in range(count):
        for k in range(lines):
            @pl.when(line == k)
            def _():
                pltpu.make_async_copy(own[c + k], raw.at[parity, c], raw_sems.at[0, c]).start()
                pltpu.make_async_copy(other[c + k], raw.at[1 - parity, c], raw_sems.at[1, c]).start()
    for step in range(SLOTS - 1):
        read(step)
    inv_ref[0] = jnp.concatenate(split2(inv_first[...]), axis=1)
    inv_ref[1] = jnp.concatenate(split2(inv_second[...]), axis=1)

    def solve_top(j):
        pltpu.make_async_copy(own[0], raw.at[parity, j], raw_sems.at[0, j]).wait()
        pltpu.make_async_copy(other[0], raw.at[1 - parity, j], raw_sems.at[1, j]).wait()
        cols = lax.broadcasted_iota(jnp.int32, (NB, width), 1)
        outer = (cols >= NB) | (first + j > 0)
        top = times_left(inv_ref[0], raw[0, j])
        top = jnp.where(outer | (grid_col > 0), -top, 0.0).astype(jnp.bfloat16)
        top_ref[:NB, :] = top
        second = raw[1, j].astype(jnp.float32) + dot(left_block[...], top)
        top = times_left(inv_ref[1], second.astype(jnp.bfloat16))
        top = jnp.where(outer | (grid_col > 1), -top, 0.0).astype(jnp.bfloat16)
        top_ref[NB:, :] = top

    def body(step, carry):
        i = step % ROW_TILES
        j = step // ROW_TILES
        slot = step % SLOTS

        @pl.when(step + SLOTS - 1 < steps)
        def _():
            read(step + SLOTS - 1)

        @pl.when(i == 0)
        def _():
            solve_top(j)

        wait_read(step)

        @pl.when(step >= SLOTS)
        def _():
            wait_write(step - SLOTS)

        rows = pl.ds(pl.multiple_of(i * tile, NB), tile)
        left = left_ref[rows, :]

        def products(start):
            cols = slice(start, min(start + NB, width))
            return dot(left[:, :NB], top_ref[:NB, cols]), dot(left[:, NB:], top_ref[NB:, cols])

        ahead = products(0)
        for start in range(0, width, NB):
            cols = slice(start, min(start + NB, width))
            first_change, second_change = ahead
            if start + NB < width:
                ahead = products(start + NB)
            value = reads[slot, :, cols].astype(jnp.float32) + first_change
            value = value.astype(jnp.bfloat16).astype(jnp.float32) + second_change
            writes[slot, :, cols] = value.astype(jnp.bfloat16)

        @pl.when((i == 0) & (grid_row == 0))
        def _():
            writes[slot, :NB, :] = -top_ref[:NB, :]

        @pl.when((i == 0) & (grid_row == 1))
        def _():
            writes[slot, :NB, :] = -top_ref[NB:, :]

        if first == 0:
            @pl.when((j == 0) & (grid_col == 0))
            def _():
                writes[slot, :, :NB] = left_ref[rows, :NB]

            @pl.when((j == 0) & (grid_col == 1))
            def _():
                writes[slot, :, :NB] = left_ref[rows, NB:]

            @pl.when((j == 0) & (i == 0) & (grid_col == 0) & (grid_row == 0))
            def _():
                writes[slot, :NB, :NB] = packed_first[...].astype(jnp.bfloat16)

            @pl.when((j == 0) & (i == 0) & (grid_col == 1) & (grid_row == 0))
            def _():
                writes[slot, :NB, :NB] = -top_ref[:NB, :NB]

            @pl.when((j == 0) & (i == 0) & (grid_col == 1) & (grid_row == 1))
            def _():
                writes[slot, :NB, :NB] = packed_second[...].astype(jnp.bfloat16)

        write(step)
        return carry

    lax.fori_loop(0, steps, body, 0)
    for step in range(steps - SLOTS, steps):
        wait_write(step)


def update_call(first, last, lines, place, matrix, left, squares, left_block, own, other, extra, before):
    rows, cols = matrix.shape
    width = cols // CHUNKS
    tile = rows // ROW_TILES
    count = last - first
    tail = list(extra) + ([] if before is None else [before])
    operands = [place, left, *squares, left_block, matrix, *own, *other, *tail]
    aliases = {} if before is None else {len(operands) - 1: 0}
    return pl.pallas_call(
        functools.partial(update_kernel, first, count, lines, len(tail)),
        out_shape=jax.ShapeDtypeStruct((rows, cols), jnp.bfloat16),
        in_specs=[smem()]
        + [vmem()] * 6
        + [hbm()]
        + [anywhere() for _ in range(len(own) + len(other) + len(extra))]
        + [hbm() for _ in tail[len(extra) :]],
        out_specs=hbm(),
        scratch_shapes=[
            pltpu.VMEM((2, count, NB, width), jnp.bfloat16),
            pltpu.VMEM((2 * NB, width), jnp.bfloat16),
            pltpu.VMEM((2, NB, 2 * NB), jnp.bfloat16),
            pltpu.VMEM((SLOTS, tile, width), jnp.bfloat16),
            pltpu.VMEM((SLOTS, tile, width), jnp.bfloat16),
            pltpu.SemaphoreType.DMA((2, count)),
            pltpu.SemaphoreType.DMA((SLOTS,)),
            pltpu.SemaphoreType.DMA((SLOTS,)),
        ],
        input_output_aliases=aliases,
        compiler_params=pltpu.CompilerParams(vmem_limit_bytes=26 * MIB),
        cost_estimate=pl.CostEstimate(
            flops=6 * rows * NB * width * count,
            bytes_accessed=6 * rows * width * count,
            transcendentals=0,
        ),
    )(*operands)


def swap(size):
    return [(i, i ^ 1) for i in range(size)]


def spread(block, axis, reach, index, size):
    stride = reach // 2
    while stride >= 2:
        pairs = [(i, i + stride) for i in range(size) if i % (2 * stride) < 2]
        moved = lax.ppermute(block, axis, pairs)
        block = jnp.where(index % (2 * stride) >= stride, moved, block)
        stride //= 2
    return block


def on_device(matrix):
    grid_rows = lax.axis_size("row")
    grid_cols = lax.axis_size("col")
    grid_row = lax.axis_index("row")
    grid_col = lax.axis_index("col")
    place = jnp.stack([grid_row, grid_col]).astype(jnp.int32)
    lines = grid_rows // 2
    width = matrix.shape[1] // CHUNKS

    diag = spread(matrix[:NB, :NB], "col", grid_cols, grid_col, grid_cols)
    diag = spread(diag, "row", grid_rows, grid_row, grid_rows)
    both_swap = [
        (i * grid_cols + j, (i ^ 1) * grid_cols + (j ^ 1))
        for i in range(grid_rows)
        for j in range(grid_cols)
    ]
    blocks = (
        diag,
        lax.ppermute(diag, "col", swap(grid_cols)),
        lax.ppermute(diag, "row", swap(grid_rows)),
        lax.ppermute(diag, ("row", "col"), both_swap),
    )

    n_ticks = CHUNKS + lines - 1
    own, other, received = [], [], []

    def move(done):
        tick = len(own)
        if tick >= n_ticks:
            return done[:1]
        if tick == 0:
            send = jnp.where(grid_row < 2, matrix[:NB, :width], diag[:1, :1])
        else:
            column = min(tick, CHUNKS - 1) * width
            send = gate_call(column, place, matrix, received[-1], [*other[-2:-1], *done])
        live = [k for k in range(lines) if 0 <= tick - k < CHUNKS]
        onward = [(2 * k + e, 2 * k + 2 + e) for k in live for e in range(2) if k + 1 < lines]
        across = [(2 * k + e, 2 * k + 1 - e) for k in live for e in range(2)]
        received.append(lax.ppermute(send, "row", onward) if onward else send)
        own.append(send)
        other.append(lax.ppermute(send, "row", across))
        return [send]

    move(blocks[2:])
    extra = []
    stride = grid_cols // 2
    column = jnp.where(grid_col < 2, matrix[:, :NB], diag[:1, :1])
    pairs = [(i, i + stride) for i in range(grid_cols) if i % (2 * stride) < 2]
    moved = lax.ppermute(column, "col", pairs)

    cost = 10**9
    per_piece = NB // W // PIECES
    kept = []
    for section in range(2):
        for piece in range(PIECES):
            if section + piece > 0:
                extra = move(square[:1])
            if section > 0 and piece == 0:
                moved = hold_call(moved, extra)
                extra = [*extra, moved]
            if piece > 0:
                body = functools.partial(next_kernel, piece * per_piece, per_piece, len(extra))
                square = factor_call(body, 3, None, square, extra, cost)
            elif section == 0:
                body = functools.partial(first_kernel, per_piece, len(extra))
                square = factor_call(body, 3, place, blocks, extra, cost)
            else:
                body = functools.partial(second_kernel, per_piece, len(extra))
                *square, left_block, top_block = factor_call(
                    body, 5, place, [*blocks, *kept[0][1:]], extra, cost
                )
        kept.append(square)

    packed, lower, upper = zip(*kept)
    column = jnp.where(grid_col % (2 * stride) >= stride, moved, column)
    column = spread(column, "col", stride, grid_col, grid_cols)
    column_other = lax.ppermute(column, "col", swap(grid_cols))
    left = left_call(place, column, column_other, *upper, top_block, move(square[:1]))
    latest = left
    out = None
    for first, last in BATCHES:
        while len(own) < min(last + lines, n_ticks):
            latest = move([latest])[0]
        sent = range(first, last + lines - 1)
        out = update_call(
            first, last, lines, place, matrix, left, (*packed, *lower), left_block,
            [own[t] for t in sent], [other[t] for t in sent], [] if latest is out else [latest], out,
        )
        latest = out
    return out


def solution(mesh):
    return jax.shard_map(
        on_device, mesh=mesh, in_specs=(P("row", "col"),), out_specs=P("row", "col"), check_vma=False
    )
```

```python
import functools

import jax
import jax.numpy as jnp
from jax import lax
from jax.experimental import pallas as pl
from jax.experimental.pallas import tpu as pltpu
from jax.sharding import PartitionSpec as P

NB = 256
W = 64
MICRO = 8
CHUNKS = 7
ROW_TILES = 7
PIECES = 2
SLOTS = 4
SPLIT = 4
BATCHES = ((0, 1), (1, 2), (2, 3), (3, 4), (4, 5), (5, 6), (6, 7))
MIB = 2**20


def split3(x):
    high = x.astype(jnp.bfloat16)
    rest = x - high.astype(jnp.float32)
    middle = rest.astype(jnp.bfloat16)
    low = (rest - middle.astype(jnp.float32)).astype(jnp.bfloat16)
    return high, middle, low


def dot(a, b):
    return jnp.dot(a, b, preferred_element_type=jnp.float32)


def factor_small(block):
    lane = lax.broadcasted_iota(jnp.int32, (W, 128), 1)
    row = lax.broadcasted_iota(jnp.int32, (W, 128), 0)
    work = jnp.where(lane < W, block, jnp.where(lane == row + W, 1.0, 0.0))
    upper = jnp.where(lane == row, 1.0, 0.0).astype(jnp.float32)
    packed = jnp.zeros((W, 128), jnp.float32)
    scale = jnp.ones((W, 128), jnp.float32)
    for first in range(0, W, MICRO):
        columns = [
            jnp.broadcast_to(work[:, j : j + 1], (W, 128)) for j in range(first, first + MICRO)
        ]
        for step in range(MICRO):
            j = first + step
            column = columns[step]
            inverse = 1.0 / column[j : j + 1, :]
            factor = jnp.where(row == j, 0.0, column * inverse)
            for later in range(step + 1, MICRO):
                other = columns[later]
                columns[later] = other - factor * other[j : j + 1, :]
            line = work[j : j + 1, :]
            below = jnp.where(row > j, factor, 0.0)
            above = factor - below
            packed = jnp.where((row == j) & (lane >= j), line, packed)
            packed = jnp.where((lane == j) & (row > j), factor, packed)
            scale = jnp.where(row == j, inverse, scale)
            work = work - jnp.where(lane < W, factor, below) * line
            upper = upper - above * upper[j : j + 1, :]
    return packed, work, upper * scale


def repeat_lanes(x, first):
    lane = lax.broadcasted_iota(jnp.int32, x.shape, 1)
    x = jnp.where((lane >= first) & (lane < first + W), x, 0.0)
    return x + pltpu.roll(x, W, 1)


def pack_left(x):
    lane = lax.broadcasted_iota(jnp.int32, x.shape, 1)
    high = x.astype(jnp.bfloat16)
    rest = x - high.astype(jnp.float32)
    middle = rest.astype(jnp.bfloat16).astype(jnp.float32)
    low = rest - middle
    second = jnp.where(lane < W, high.astype(jnp.float32), middle).astype(jnp.bfloat16)
    third = jnp.where(lane < W, middle, low).astype(jnp.bfloat16)
    return jnp.concatenate([high, second, third], axis=1)


def pack_right(x):
    high, middle, low = split3(x)
    return jnp.concatenate([high, middle, low, high, middle, high], axis=0)


def block_step(k, work_ref, lower_ref, upper_ref):
    active = NB - W * k
    packed, left_small, upper_small = factor_small(work_ref[:W, :128])
    small_left = pack_left(repeat_lanes(left_small, W))
    small_upper = pack_right(repeat_lanes(upper_small, 0))

    work = work_ref[...]
    lower = lower_ref[...]
    upper = upper_ref[...]
    col = lax.broadcasted_iota(jnp.int32, (W, NB), 1)
    row = lax.broadcasted_iota(jnp.int32, (NB, 128), 0)
    lane = lax.broadcasted_iota(jnp.int32, (NB, 128), 1)
    live_col = (col >= W) & (col < active)
    live_row = (row >= W) & (row < active)

    tops = dot(small_left, pack_right(jnp.concatenate([work[:W], lower[:W]], axis=1)))
    top, lower_top = tops[:, :NB], tops[:, NB:]
    sides = jnp.concatenate([work[:, :128], upper[:, :128]], axis=0)
    sides = dot(pack_left(repeat_lanes(sides, 0)), small_upper)
    left, upper_left = sides[:NB], sides[NB:]
    left_live = jnp.where(live_row, left, 0.0)
    top_live = jnp.where(live_col, top, 0.0)

    right_packed = pack_right(jnp.concatenate([top_live, lower_top], axis=1))
    change = dot(pack_left(left_live), right_packed)
    upper_change = dot(pack_left(upper_left), right_packed[:, :NB])
    work_new = work - change[:, :NB]
    lower_new = lower - change[:, NB:]
    upper_new = upper - upper_change

    left_side = jnp.where((lane < W) & live_row, left, work_new[:, :128])
    work_new = jnp.concatenate([left_side, work_new[:, 128:]], axis=1)
    packed_wide = jnp.concatenate([packed, jnp.zeros_like(packed)], axis=1)
    top_new = jnp.where(col < W, packed_wide, jnp.where(live_col, top, work[:W]))
    work_new = jnp.concatenate([work_new[W:], top_new], axis=0)
    work_ref[...] = pltpu.roll(work_new, NB - W, 1)
    lower_ref[...] = jnp.concatenate([lower_new[W:], lower_top], axis=0)
    upper_side = jnp.where(lane < W, upper_left, upper_new[:, :128])
    upper_ref[...] = pltpu.roll(
        jnp.concatenate([upper_side, upper_new[:, 128:]], axis=1), NB - W, 1
    )


def identity():
    row = lax.broadcasted_iota(jnp.int32, (NB, NB), 0)
    col = lax.broadcasted_iota(jnp.int32, (NB, NB), 1)
    return jnp.where(row == col, 1.0, 0.0).astype(jnp.float32)


def split2(x):
    high = x.astype(jnp.bfloat16)
    return high, (x - high.astype(jnp.float32)).astype(jnp.bfloat16)


def times_right(a, b):
    return dot(jnp.concatenate([a, a], axis=1), jnp.concatenate(split2(b), axis=0))


def times_left(a, b):
    return dot(a, jnp.concatenate([b, b], axis=0))


def run_steps(first, count, work_ref, lower_ref, upper_ref):
    def body(k, carry):
        block_step(k, work_ref, lower_ref, upper_ref)
        return carry

    lax.fori_loop(first, first + count, body, 0)


def pick(place_ref, blocks, i, j):
    same_row = place_ref[0] % 2 == i
    same_col = place_ref[1] % 2 == j
    own, across, below, both = [block[...].astype(jnp.float32) for block in blocks]
    near = jnp.where(same_col, own, across)
    far = jnp.where(same_col, below, both)
    return jnp.where(same_row, near, far)


def first_kernel(count, n_extra, place_ref, d0, d1, d2, d3, *refs):
    work_ref, lower_ref, upper_ref = refs[n_extra:][:3]
    work_ref[...] = pick(place_ref, (d0, d1, d2, d3), 0, 0)
    lower_ref[...] = identity()
    upper_ref[...] = identity()
    run_steps(0, count, work_ref, lower_ref, upper_ref)


def second_kernel(count, n_extra, place_ref, d0, d1, d2, d3, inv_lower, inv_upper, *refs):
    work_ref, lower_ref, upper_ref, left_ref, top_ref = refs[n_extra:][:5]
    blocks = (d0, d1, d2, d3)
    left = times_right(pick(place_ref, blocks, 1, 0).astype(jnp.bfloat16), inv_upper[...])
    left = left.astype(jnp.bfloat16)
    top = times_left(jnp.concatenate(split2(inv_lower[...]), axis=1), pick(place_ref, blocks, 0, 1).astype(jnp.bfloat16))
    top = top.astype(jnp.bfloat16)
    left_ref[...] = left
    top_ref[...] = top
    block = pick(place_ref, blocks, 1, 1) - dot(left, top)
    work_ref[...] = block.astype(jnp.bfloat16).astype(jnp.float32)
    lower_ref[...] = identity()
    upper_ref[...] = identity()
    run_steps(0, count, work_ref, lower_ref, upper_ref)


def next_kernel(first, count, n_extra, work_in, lower_in, upper_in, *refs):
    work_ref, lower_ref, upper_ref = refs[n_extra:][:3]
    work_ref[...] = work_in[...]
    lower_ref[...] = lower_in[...]
    upper_ref[...] = upper_in[...]
    run_steps(first, count, work_ref, lower_ref, upper_ref)


def vmem():
    return pl.BlockSpec(memory_space=pltpu.VMEM)


def smem():
    return pl.BlockSpec(memory_space=pltpu.SMEM)


def hbm():
    return pl.BlockSpec(memory_space=pltpu.HBM)


def anywhere():
    return pl.BlockSpec(memory_space=pl.ANY)


def factor_call(body, n_out, place, operands, extra, flops):
    square = jax.ShapeDtypeStruct((NB, NB), jnp.float32)
    panel = jax.ShapeDtypeStruct((NB, NB), jnp.bfloat16)
    scalars = [] if place is None else [place]
    return pl.pallas_call(
        body,
        out_shape=[square] * 3 + [panel] * (n_out - 3),
        in_specs=[smem() for _ in scalars] + [vmem() for _ in operands] + [anywhere() for _ in extra],
        out_specs=[vmem()] * n_out,
        compiler_params=pltpu.CompilerParams(vmem_limit_bytes=10 * MIB),
        cost_estimate=pl.CostEstimate(flops=flops, bytes_accessed=2**21, transcendentals=0),
    )(*scalars, *operands, *extra)


def gate_kernel(column, place_ref, received, matrix, *refs):
    out, sem = refs[-2:]

    @pl.when(place_ref[0] < 2)
    def _():
        copy = pltpu.make_async_copy(
            matrix.at[pl.ds(0, NB), pl.ds(column, out.shape[1])], out, sem
        )
        copy.start()
        copy.wait()

    @pl.when(place_ref[0] >= 2)
    def _():
        out[...] = received[...]


def gate_call(column, place, matrix, received, before):
    return pl.pallas_call(
        functools.partial(gate_kernel, column),
        out_shape=jax.ShapeDtypeStruct(received.shape, received.dtype),
        in_specs=[smem(), vmem(), hbm()] + [anywhere() for _ in before],
        out_specs=vmem(),
        scratch_shapes=[pltpu.SemaphoreType.DMA(())],
        compiler_params=pltpu.CompilerParams(vmem_limit_bytes=24 * MIB),
    )(place, received, matrix, *before)


def hold_kernel(*refs):
    pass


def hold_call(value, before):
    return pl.pallas_call(
        hold_kernel,
        out_shape=jax.ShapeDtypeStruct(value.shape, value.dtype),
        in_specs=[anywhere() for _ in range(1 + len(before))],
        out_specs=anywhere(),
        input_output_aliases={0: 0},
        compiler_params=pltpu.CompilerParams(vmem_limit_bytes=MIB),
    )(value, *before)


def left_kernel(place_ref, own, other, inv_first, inv_second, top, *refs):
    out = refs[-1]
    parity = place_ref[1] % 2
    own_value = own[...].astype(jnp.float32)
    other_value = other[...].astype(jnp.float32)
    first = jnp.where(parity == 0, own_value, other_value).astype(jnp.bfloat16)
    second = jnp.where(parity == 0, other_value, own_value)
    rows = lax.broadcasted_iota(jnp.int32, (own.shape[0], NB), 0)
    outer = (rows >= NB) | (pl.program_id(0) > 0)
    left = times_right(first, inv_first[...])
    left = jnp.where(outer | (place_ref[0] > 0), left, 0.0).astype(jnp.bfloat16)
    out[:, :NB] = left
    second = (second - dot(left, top[...])).astype(jnp.bfloat16)
    left = times_right(second, inv_second[...])
    left = jnp.where(outer | (place_ref[0] > 1), left, 0.0).astype(jnp.bfloat16)
    out[:, NB:] = left


def left_call(place, own, other, inv_first, inv_second, top, extra):
    rows = own.shape[0]
    tile = rows // 4
    whole = pl.BlockSpec((NB, NB), lambda i: (0, 0))
    return pl.pallas_call(
        left_kernel,
        grid=(4,),
        out_shape=jax.ShapeDtypeStruct((rows, 2 * NB), jnp.bfloat16),
        in_specs=[
            smem(),
            pl.BlockSpec((tile, NB), lambda i: (i, 0)),
            pl.BlockSpec((tile, NB), lambda i: (i, 0)),
            whole,
            whole,
            whole,
        ]
        + [anywhere() for _ in extra],
        out_specs=pl.BlockSpec((tile, 2 * NB), lambda i: (i, 0)),
        compiler_params=pltpu.CompilerParams(vmem_limit_bytes=12 * MIB),
        cost_estimate=pl.CostEstimate(
            flops=14 * rows * NB * NB, bytes_accessed=8 * rows * NB, transcendentals=0
        ),
    )(place, own, other, inv_first, inv_second, top, *extra)


def update_kernel(first, count, lines, n_extra, place_ref, left_ref, packed_first, packed_second,
                  inv_first, inv_second, left_block, matrix, *refs):
    n_sent = count + lines - 1
    own = refs[:n_sent]
    other = refs[n_sent : 2 * n_sent]
    out, raw, top_ref, inv_ref, reads, writes, raw_sems, read_sems, write_sems = refs[2 * n_sent + n_extra :]
    grid_row = place_ref[0]
    grid_col = place_ref[1]
    line = grid_row // 2
    parity = grid_row % 2
    tile, width = reads.shape[1:]
    steps = count * ROW_TILES
    part = tile // SPLIT

    def window(step, begin, size):
        top = pl.multiple_of(step % ROW_TILES * tile + begin, 16)
        side = pl.multiple_of((first + step // ROW_TILES) * width, 128)
        return pl.ds(top, size), pl.ds(side, width)

    def read(step):
        slot = step % SLOTS
        for n in range(SPLIT):
            pltpu.make_async_copy(
                matrix.at[window(step, n * part, part)],
                reads.at[slot, pl.ds(n * part, part)],
                read_sems.at[slot],
            ).start()

    def wait_read(step):
        slot = step % SLOTS
        pltpu.make_async_copy(matrix.at[window(step, 0, tile)], reads.at[slot], read_sems.at[slot]).wait()

    def write(step):
        slot = step % SLOTS
        for n in range(SPLIT):
            pltpu.make_async_copy(
                writes.at[slot, pl.ds(n * part, part)],
                out.at[window(step, n * part, part)],
                write_sems.at[slot],
            ).start()

    def wait_write(step):
        slot = step % SLOTS
        pltpu.make_async_copy(writes.at[slot], out.at[window(step, 0, tile)], write_sems.at[slot]).wait()

    for c in range(count):
        for k in range(lines):
            @pl.when(line == k)
            def _():
                pltpu.make_async_copy(own[c + k], raw.at[parity, c], raw_sems.at[0, c]).start()
                pltpu.make_async_copy(other[c + k], raw.at[1 - parity, c], raw_sems.at[1, c]).start()
    for step in range(SLOTS - 1):
        read(step)
    inv_ref[0] = jnp.concatenate(split2(inv_first[...]), axis=1)
    inv_ref[1] = jnp.concatenate(split2(inv_second[...]), axis=1)

    def solve_top(j):
        pltpu.make_async_copy(own[0], raw.at[parity, j], raw_sems.at[0, j]).wait()
        pltpu.make_async_copy(other[0], raw.at[1 - parity, j], raw_sems.at[1, j]).wait()
        cols = lax.broadcasted_iota(jnp.int32, (NB, width), 1)
        outer = (cols >= NB) | (first + j > 0)
        top = times_left(inv_ref[0], raw[0, j])
        top = jnp.where(outer | (grid_col > 0), -top, 0.0).astype(jnp.bfloat16)
        top_ref[:NB, :] = top
        second = raw[1, j].astype(jnp.float32) + dot(left_block[...], top)
        top = times_left(inv_ref[1], second.astype(jnp.bfloat16))
        top = jnp.where(outer | (grid_col > 1), -top, 0.0).astype(jnp.bfloat16)
        top_ref[NB:, :] = top

    def body(step, carry):
        i = step % ROW_TILES
        j = step // ROW_TILES
        slot = step % SLOTS

        @pl.when(step + SLOTS - 1 < steps)
        def _():
            read(step + SLOTS - 1)

        @pl.when(i == 0)
        def _():
            solve_top(j)

        wait_read(step)

        @pl.when(step >= SLOTS)
        def _():
            wait_write(step - SLOTS)

        rows = pl.ds(pl.multiple_of(i * tile, NB), tile)
        left = left_ref[rows, :]

        def products(start):
            cols = slice(start, min(start + NB, width))
            return dot(left[:, :NB], top_ref[:NB, cols]), dot(left[:, NB:], top_ref[NB:, cols])

        ahead = products(0)
        for start in range(0, width, NB):
            cols = slice(start, min(start + NB, width))
            first_change, second_change = ahead
            if start + NB < width:
                ahead = products(start + NB)
            value = reads[slot, :, cols].astype(jnp.float32) + first_change
            value = value.astype(jnp.bfloat16).astype(jnp.float32) + second_change
            writes[slot, :, cols] = value.astype(jnp.bfloat16)

        @pl.when((i == 0) & (grid_row == 0))
        def _():
            writes[slot, :NB, :] = -top_ref[:NB, :]

        @pl.when((i == 0) & (grid_row == 1))
        def _():
            writes[slot, :NB, :] = -top_ref[NB:, :]

        if first == 0:
            @pl.when((j == 0) & (grid_col == 0))
            def _():
                writes[slot, :, :NB] = left_ref[rows, :NB]

            @pl.when((j == 0) & (grid_col == 1))
            def _():
                writes[slot, :, :NB] = left_ref[rows, NB:]

            @pl.when((j == 0) & (i == 0) & (grid_col == 0) & (grid_row == 0))
            def _():
                writes[slot, :NB, :NB] = packed_first[...].astype(jnp.bfloat16)

            @pl.when((j == 0) & (i == 0) & (grid_col == 1) & (grid_row == 0))
            def _():
                writes[slot, :NB, :NB] = -top_ref[:NB, :NB]

            @pl.when((j == 0) & (i == 0) & (grid_col == 1) & (grid_row == 1))
            def _():
                writes[slot, :NB, :NB] = packed_second[...].astype(jnp.bfloat16)

        write(step)
        return carry

    lax.fori_loop(0, steps, body, 0)
    for step in range(steps - SLOTS, steps):
        wait_write(step)


def update_call(first, last, lines, place, matrix, left, squares, left_block, own, other, extra, before):
    rows, cols = matrix.shape
    width = cols // CHUNKS
    tile = rows // ROW_TILES
    count = last - first
    tail = list(extra) + ([] if before is None else [before])
    operands = [place, left, *squares, left_block, matrix, *own, *other, *tail]
    aliases = {} if before is None else {len(operands) - 1: 0}
    return pl.pallas_call(
        functools.partial(update_kernel, first, count, lines, len(tail)),
        out_shape=jax.ShapeDtypeStruct((rows, cols), jnp.bfloat16),
        in_specs=[smem()]
        + [vmem()] * 6
        + [hbm()]
        + [anywhere() for _ in range(len(own) + len(other) + len(extra))]
        + [hbm() for _ in tail[len(extra) :]],
        out_specs=hbm(),
        scratch_shapes=[
            pltpu.VMEM((2, count, NB, width), jnp.bfloat16),
            pltpu.VMEM((2 * NB, width), jnp.bfloat16),
            pltpu.VMEM((2, NB, 2 * NB), jnp.bfloat16),
            pltpu.VMEM((SLOTS, tile, width), jnp.bfloat16),
            pltpu.VMEM((SLOTS, tile, width), jnp.bfloat16),
            pltpu.SemaphoreType.DMA((2, count)),
            pltpu.SemaphoreType.DMA((SLOTS,)),
            pltpu.SemaphoreType.DMA((SLOTS,)),
        ],
        input_output_aliases=aliases,
        compiler_params=pltpu.CompilerParams(vmem_limit_bytes=26 * MIB),
        cost_estimate=pl.CostEstimate(
            flops=6 * rows * NB * width * count,
            bytes_accessed=6 * rows * width * count,
            transcendentals=0,
        ),
    )(*operands)


def swap(size):
    return [(i, i ^ 1) for i in range(size)]


def spread(block, axis, reach, index, size):
    stride = reach // 2
    while stride >= 2:
        pairs = [(i, i + stride) for i in range(size) if i % (2 * stride) < 2]
        moved = lax.ppermute(block, axis, pairs)
        block = jnp.where(index % (2 * stride) >= stride, moved, block)
        stride //= 2
    return block


def on_device(matrix):
    grid_rows = lax.axis_size("row")
    grid_cols = lax.axis_size("col")
    grid_row = lax.axis_index("row")
    grid_col = lax.axis_index("col")
    place = jnp.stack([grid_row, grid_col]).astype(jnp.int32)
    lines = grid_rows // 2
    width = matrix.shape[1] // CHUNKS

    diag = spread(matrix[:NB, :NB], "col", grid_cols, grid_col, grid_cols)
    half = grid_rows // 2
    pairs = [(i, i + half) for i in range(2)]
    diag = jnp.where(grid_row >= half, lax.ppermute(diag, "row", pairs), diag)
    near = diag[:1, :1]
    diag = spread(diag, "row", half, grid_row, grid_rows)
    both_swap = [
        (i * grid_cols + j, (i ^ 1) * grid_cols + (j ^ 1))
        for i in range(grid_rows)
        for j in range(grid_cols)
    ]
    blocks = (
        diag,
        lax.ppermute(diag, "col", swap(grid_cols)),
        lax.ppermute(diag, "row", swap(grid_rows)),
        lax.ppermute(diag, ("row", "col"), both_swap),
    )

    n_ticks = CHUNKS + lines - 1
    own, other, received = [], [], []

    def move(done):
        tick = len(own)
        if tick >= n_ticks:
            return done[:1]
        if tick == 0:
            send = matrix[:NB, :width]
        else:
            column = min(tick, CHUNKS - 1) * width
            send = gate_call(column, place, matrix, received[-1], [*other[-2:-1], *done])
        live = [k for k in range(lines) if 0 <= tick - k < CHUNKS]
        onward = [(2 * k + e, 2 * k + 2 + e) for k in live for e in range(2) if k + 1 < lines]
        across = [(2 * k + e, 2 * k + 1 - e) for k in live for e in range(2)]
        received.append(lax.ppermute(send, "row", onward) if onward else send)
        own.append(send)
        other.append(lax.ppermute(send, "row", across))
        return [send]

    move([])
    extra = move(blocks[1:])
    stride = grid_cols // 2
    column = jnp.where(grid_col < 2, matrix[:, :NB], near)
    pairs = [(i, i + stride) for i in range(grid_cols) if i % (2 * stride) < 2]
    moved = lax.ppermute(column, "col", pairs)

    cost = 10**9
    per_piece = NB // W // PIECES
    kept = []
    for section in range(2):
        for piece in range(PIECES):
            if section > 0 and piece == 0:
                extra = move(square[:1])
                moved = hold_call(moved, extra)
                extra = [*extra, moved]
            if piece > 0:
                extra = []
                body = functools.partial(next_kernel, piece * per_piece, per_piece, len(extra))
                square = factor_call(body, 3, None, square, extra, cost)
            elif section == 0:
                body = functools.partial(first_kernel, per_piece, len(extra))
                square = factor_call(body, 3, place, blocks, extra, cost)
            else:
                body = functools.partial(second_kernel, per_piece, len(extra))
                *square, left_block, top_block = factor_call(
                    body, 5, place, [*blocks, *kept[0][1:]], extra, cost
                )
        kept.append(square)

    packed, lower, upper = zip(*kept)
    column = jnp.where(grid_col % (2 * stride) >= stride, moved, column)
    column = spread(column, "col", stride, grid_col, grid_cols)
    column_other = lax.ppermute(column, "col", swap(grid_cols))
    left = left_call(place, column, column_other, *upper, top_block, move(square[:1]))
    latest = left
    out = None
    for first, last in BATCHES:
        while len(own) < min(last + lines, n_ticks):
            latest = move([latest])[0]
        sent = range(first, last + lines - 1)
        out = update_call(
            first, last, lines, place, matrix, left, (*packed, *lower), left_block,
            [own[t] for t in sent], [other[t] for t in sent], [] if latest is out else [latest], out,
        )
        latest = out
    return out


def solution(mesh):
    return jax.shard_map(
        on_device, mesh=mesh, in_specs=(P("row", "col"),), out_specs=P("row", "col"), check_vma=False
    )
```

```python
import functools

import jax
import jax.numpy as jnp
from jax import lax
from jax.experimental import pallas as pl
from jax.experimental.pallas import tpu as pltpu
from jax.sharding import PartitionSpec as P

NB = 256
W = 64
MICRO = 8
CHUNKS = 7
ROW_TILES = 7
PIECES = 2
SLOTS = 4
SPLIT = 4
BATCHES = ((0, 1), (1, 2), (2, 3), (3, 4), (4, 5), (5, 6), (6, 7))
MIB = 2**20


def split3(x):
    high = x.astype(jnp.bfloat16)
    rest = x - high.astype(jnp.float32)
    middle = rest.astype(jnp.bfloat16)
    low = (rest - middle.astype(jnp.float32)).astype(jnp.bfloat16)
    return high, middle, low


def dot(a, b):
    return jnp.dot(a, b, preferred_element_type=jnp.float32)


def factor_small(block):
    lane = lax.broadcasted_iota(jnp.int32, (W, 128), 1)
    row = lax.broadcasted_iota(jnp.int32, (W, 128), 0)
    work = jnp.where(lane < W, block, jnp.where(lane == row + W, 1.0, 0.0))
    upper = jnp.where(lane == row, 1.0, 0.0).astype(jnp.float32)
    packed = jnp.zeros((W, 128), jnp.float32)
    scale = jnp.ones((W, 128), jnp.float32)
    for first in range(0, W, MICRO):
        columns = [
            jnp.broadcast_to(work[:, j : j + 1], (W, 128)) for j in range(first, first + MICRO)
        ]
        for step in range(MICRO):
            j = first + step
            column = columns[step]
            inverse = 1.0 / column[j : j + 1, :]
            factor = jnp.where(row == j, 0.0, column * inverse)
            for later in range(step + 1, MICRO):
                other = columns[later]
                columns[later] = other - factor * other[j : j + 1, :]
            line = work[j : j + 1, :]
            below = jnp.where(row > j, factor, 0.0)
            above = factor - below
            packed = jnp.where((row == j) & (lane >= j), line, packed)
            packed = jnp.where((lane == j) & (row > j), factor, packed)
            scale = jnp.where(row == j, inverse, scale)
            work = work - jnp.where(lane < W, factor, below) * line
            upper = upper - above * upper[j : j + 1, :]
    return packed, work, upper * scale


def repeat_lanes(x, first):
    lane = lax.broadcasted_iota(jnp.int32, x.shape, 1)
    x = jnp.where((lane >= first) & (lane < first + W), x, 0.0)
    return x + pltpu.roll(x, W, 1)


def pack_left(x):
    lane = lax.broadcasted_iota(jnp.int32, x.shape, 1)
    high = x.astype(jnp.bfloat16)
    rest = x - high.astype(jnp.float32)
    middle = rest.astype(jnp.bfloat16).astype(jnp.float32)
    low = rest - middle
    second = jnp.where(lane < W, high.astype(jnp.float32), middle).astype(jnp.bfloat16)
    third = jnp.where(lane < W, middle, low).astype(jnp.bfloat16)
    return jnp.concatenate([high, second, third], axis=1)


def pack_right(x):
    high, middle, low = split3(x)
    return jnp.concatenate([high, middle, low, high, middle, high], axis=0)


def block_step(k, work_ref, lower_ref, upper_ref):
    active = NB - W * k
    packed, left_small, upper_small = factor_small(work_ref[:W, :128])
    small_left = pack_left(repeat_lanes(left_small, W))
    small_upper = pack_right(repeat_lanes(upper_small, 0))

    work = work_ref[...]
    lower = lower_ref[...]
    upper = upper_ref[...]
    col = lax.broadcasted_iota(jnp.int32, (W, NB), 1)
    row = lax.broadcasted_iota(jnp.int32, (NB, 128), 0)
    lane = lax.broadcasted_iota(jnp.int32, (NB, 128), 1)
    live_col = (col >= W) & (col < active)
    live_row = (row >= W) & (row < active)

    tops = dot(small_left, pack_right(jnp.concatenate([work[:W], lower[:W]], axis=1)))
    top, lower_top = tops[:, :NB], tops[:, NB:]
    sides = jnp.concatenate([work[:, :128], upper[:, :128]], axis=0)
    sides = dot(pack_left(repeat_lanes(sides, 0)), small_upper)
    left, upper_left = sides[:NB], sides[NB:]
    left_live = jnp.where(live_row, left, 0.0)
    top_live = jnp.where(live_col, top, 0.0)

    right_packed = pack_right(jnp.concatenate([top_live, lower_top], axis=1))
    change = dot(pack_left(left_live), right_packed)
    upper_change = dot(pack_left(upper_left), right_packed[:, :NB])
    work_new = work - change[:, :NB]
    lower_new = lower - change[:, NB:]
    upper_new = upper - upper_change

    left_side = jnp.where((lane < W) & live_row, left, work_new[:, :128])
    work_new = jnp.concatenate([left_side, work_new[:, 128:]], axis=1)
    packed_wide = jnp.concatenate([packed, jnp.zeros_like(packed)], axis=1)
    top_new = jnp.where(col < W, packed_wide, jnp.where(live_col, top, work[:W]))
    work_new = jnp.concatenate([work_new[W:], top_new], axis=0)
    work_ref[...] = pltpu.roll(work_new, NB - W, 1)
    lower_ref[...] = jnp.concatenate([lower_new[W:], lower_top], axis=0)
    upper_side = jnp.where(lane < W, upper_left, upper_new[:, :128])
    upper_ref[...] = pltpu.roll(
        jnp.concatenate([upper_side, upper_new[:, 128:]], axis=1), NB - W, 1
    )


def identity():
    row = lax.broadcasted_iota(jnp.int32, (NB, NB), 0)
    col = lax.broadcasted_iota(jnp.int32, (NB, NB), 1)
    return jnp.where(row == col, 1.0, 0.0).astype(jnp.float32)


def split2(x):
    high = x.astype(jnp.bfloat16)
    return high, (x - high.astype(jnp.float32)).astype(jnp.bfloat16)


def times_right(a, b):
    return dot(jnp.concatenate([a, a], axis=1), jnp.concatenate(split2(b), axis=0))


def times_left(a, b):
    return dot(a, jnp.concatenate([b, b], axis=0))


def run_steps(first, count, work_ref, lower_ref, upper_ref):
    def body(k, carry):
        block_step(k, work_ref, lower_ref, upper_ref)
        return carry

    lax.fori_loop(first, first + count, body, 0)


def pick(place_ref, blocks, i, j):
    same_row = place_ref[0] % 2 == i
    same_col = place_ref[1] % 2 == j
    own, across, below, both = [block[...].astype(jnp.float32) for block in blocks]
    near = jnp.where(same_col, own, across)
    far = jnp.where(same_col, below, both)
    return jnp.where(same_row, near, far)


def first_kernel(count, n_extra, place_ref, d0, d1, d2, d3, *refs):
    work_ref, lower_ref, upper_ref = refs[n_extra:][:3]
    work_ref[...] = pick(place_ref, (d0, d1, d2, d3), 0, 0)
    lower_ref[...] = identity()
    upper_ref[...] = identity()
    run_steps(0, count, work_ref, lower_ref, upper_ref)


def second_kernel(count, n_extra, place_ref, d0, d1, d2, d3, inv_lower, inv_upper, *refs):
    work_ref, lower_ref, upper_ref, left_ref, top_ref = refs[n_extra:][:5]
    blocks = (d0, d1, d2, d3)
    left = times_right(pick(place_ref, blocks, 1, 0).astype(jnp.bfloat16), inv_upper[...])
    left = left.astype(jnp.bfloat16)
    top = times_left(jnp.concatenate(split2(inv_lower[...]), axis=1), pick(place_ref, blocks, 0, 1).astype(jnp.bfloat16))
    top = top.astype(jnp.bfloat16)
    left_ref[...] = left
    top_ref[...] = top
    block = pick(place_ref, blocks, 1, 1) - dot(left, top)
    work_ref[...] = block.astype(jnp.bfloat16).astype(jnp.float32)
    lower_ref[...] = identity()
    upper_ref[...] = identity()
    run_steps(0, count, work_ref, lower_ref, upper_ref)


def next_kernel(first, count, n_extra, work_in, lower_in, upper_in, *refs):
    work_ref, lower_ref, upper_ref = refs[n_extra:][:3]
    work_ref[...] = work_in[...]
    lower_ref[...] = lower_in[...]
    upper_ref[...] = upper_in[...]
    run_steps(first, count, work_ref, lower_ref, upper_ref)


def vmem():
    return pl.BlockSpec(memory_space=pltpu.VMEM)


def smem():
    return pl.BlockSpec(memory_space=pltpu.SMEM)


def hbm():
    return pl.BlockSpec(memory_space=pltpu.HBM)


def anywhere():
    return pl.BlockSpec(memory_space=pl.ANY)


def factor_call(body, n_out, place, operands, extra, flops):
    square = jax.ShapeDtypeStruct((NB, NB), jnp.float32)
    panel = jax.ShapeDtypeStruct((NB, NB), jnp.bfloat16)
    scalars = [] if place is None else [place]
    return pl.pallas_call(
        body,
        out_shape=[square] * 3 + [panel] * (n_out - 3),
        in_specs=[smem() for _ in scalars] + [vmem() for _ in operands] + [anywhere() for _ in extra],
        out_specs=[vmem()] * n_out,
        compiler_params=pltpu.CompilerParams(vmem_limit_bytes=10 * MIB),
        cost_estimate=pl.CostEstimate(flops=flops, bytes_accessed=2**21, transcendentals=0),
    )(*scalars, *operands, *extra)


def gate_kernel(column, place_ref, received, matrix, *refs):
    out, sem = refs[-2:]

    @pl.when(place_ref[0] < 2)
    def _():
        copy = pltpu.make_async_copy(
            matrix.at[pl.ds(0, NB), pl.ds(column, out.shape[1])], out, sem
        )
        copy.start()
        copy.wait()

    @pl.when(place_ref[0] >= 2)
    def _():
        out[...] = received[...]


def gate_call(column, place, matrix, received, before):
    return pl.pallas_call(
        functools.partial(gate_kernel, column),
        out_shape=jax.ShapeDtypeStruct(received.shape, received.dtype),
        in_specs=[smem(), vmem(), hbm()] + [anywhere() for _ in before],
        out_specs=vmem(),
        scratch_shapes=[pltpu.SemaphoreType.DMA(())],
        compiler_params=pltpu.CompilerParams(vmem_limit_bytes=24 * MIB),
    )(place, received, matrix, *before)


def hold_kernel(*refs):
    pass


def hold_call(value, before):
    return pl.pallas_call(
        hold_kernel,
        out_shape=jax.ShapeDtypeStruct(value.shape, value.dtype),
        in_specs=[anywhere() for _ in range(1 + len(before))],
        out_specs=anywhere(),
        input_output_aliases={0: 0},
        compiler_params=pltpu.CompilerParams(vmem_limit_bytes=MIB),
    )(value, *before)


def left_kernel(place_ref, own, other, inv_first, inv_second, top, *refs):
    out = refs[-1]
    parity = place_ref[1] % 2
    own_value = own[...].astype(jnp.float32)
    other_value = other[...].astype(jnp.float32)
    first = jnp.where(parity == 0, own_value, other_value).astype(jnp.bfloat16)
    second = jnp.where(parity == 0, other_value, own_value)
    rows = lax.broadcasted_iota(jnp.int32, (own.shape[0], NB), 0)
    outer = (rows >= NB) | (pl.program_id(0) > 0)
    left = times_right(first, inv_first[...])
    left = jnp.where(outer | (place_ref[0] > 0), left, 0.0).astype(jnp.bfloat16)
    out[:, :NB] = left
    second = (second - dot(left, top[...])).astype(jnp.bfloat16)
    left = times_right(second, inv_second[...])
    left = jnp.where(outer | (place_ref[0] > 1), left, 0.0).astype(jnp.bfloat16)
    out[:, NB:] = left


def left_call(place, own, other, inv_first, inv_second, top, extra):
    rows = own.shape[0]
    tile = rows // 4
    whole = pl.BlockSpec((NB, NB), lambda i: (0, 0))
    return pl.pallas_call(
        left_kernel,
        grid=(4,),
        out_shape=jax.ShapeDtypeStruct((rows, 2 * NB), jnp.bfloat16),
        in_specs=[
            smem(),
            pl.BlockSpec((tile, NB), lambda i: (i, 0)),
            pl.BlockSpec((tile, NB), lambda i: (i, 0)),
            whole,
            whole,
            whole,
        ]
        + [anywhere() for _ in extra],
        out_specs=pl.BlockSpec((tile, 2 * NB), lambda i: (i, 0)),
        compiler_params=pltpu.CompilerParams(vmem_limit_bytes=12 * MIB),
        cost_estimate=pl.CostEstimate(
            flops=14 * rows * NB * NB, bytes_accessed=8 * rows * NB, transcendentals=0
        ),
    )(place, own, other, inv_first, inv_second, top, *extra)


def update_kernel(first, count, lines, n_extra, place_ref, left_ref, packed_first, packed_second,
                  inv_first, inv_second, left_block, matrix, *refs):
    n_sent = count + lines - 1
    own = refs[:n_sent]
    other = refs[n_sent : 2 * n_sent]
    out, raw, top_ref, inv_ref, reads, writes, raw_sems, read_sems, write_sems = refs[2 * n_sent + n_extra :]
    grid_row = place_ref[0]
    grid_col = place_ref[1]
    line = grid_row // 2
    parity = grid_row % 2
    tile, width = reads.shape[1:]
    steps = count * ROW_TILES
    part = tile // SPLIT

    def window(step, begin, size):
        top = pl.multiple_of(step % ROW_TILES * tile + begin, 16)
        side = pl.multiple_of((first + step // ROW_TILES) * width, 128)
        return pl.ds(top, size), pl.ds(side, width)

    def read(step):
        slot = step % SLOTS
        for n in range(SPLIT):
            pltpu.make_async_copy(
                matrix.at[window(step, n * part, part)],
                reads.at[slot, pl.ds(n * part, part)],
                read_sems.at[slot],
            ).start()

    def wait_read(step):
        slot = step % SLOTS
        pltpu.make_async_copy(matrix.at[window(step, 0, tile)], reads.at[slot], read_sems.at[slot]).wait()

    def write(step):
        slot = step % SLOTS
        for n in range(SPLIT):
            pltpu.make_async_copy(
                writes.at[slot, pl.ds(n * part, part)],
                out.at[window(step, n * part, part)],
                write_sems.at[slot],
            ).start()

    def wait_write(step):
        slot = step % SLOTS
        pltpu.make_async_copy(writes.at[slot], out.at[window(step, 0, tile)], write_sems.at[slot]).wait()

    for c in range(count):
        for k in range(lines):
            @pl.when(line == k)
            def _():
                pltpu.make_async_copy(own[c + k], raw.at[parity, c], raw_sems.at[0, c]).start()
                pltpu.make_async_copy(other[c + k], raw.at[1 - parity, c], raw_sems.at[1, c]).start()
    for step in range(SLOTS - 1):
        read(step)
    inv_ref[0] = jnp.concatenate(split2(inv_first[...]), axis=1)
    inv_ref[1] = jnp.concatenate(split2(inv_second[...]), axis=1)

    def solve_top(j):
        pltpu.make_async_copy(own[0], raw.at[parity, j], raw_sems.at[0, j]).wait()
        pltpu.make_async_copy(other[0], raw.at[1 - parity, j], raw_sems.at[1, j]).wait()
        cols = lax.broadcasted_iota(jnp.int32, (NB, width), 1)
        outer = (cols >= NB) | (first + j > 0)
        top = times_left(inv_ref[0], raw[0, j])
        top = jnp.where(outer | (grid_col > 0), -top, 0.0).astype(jnp.bfloat16)
        top_ref[:NB, :] = top
        second = raw[1, j].astype(jnp.float32) + dot(left_block[...], top)
        top = times_left(inv_ref[1], second.astype(jnp.bfloat16))
        top = jnp.where(outer | (grid_col > 1), -top, 0.0).astype(jnp.bfloat16)
        top_ref[NB:, :] = top

    def body(step, carry):
        i = step % ROW_TILES
        j = step // ROW_TILES
        slot = step % SLOTS

        @pl.when(step + SLOTS - 1 < steps)
        def _():
            read(step + SLOTS - 1)

        @pl.when(i == 0)
        def _():
            solve_top(j)

        wait_read(step)

        @pl.when(step >= SLOTS)
        def _():
            wait_write(step - SLOTS)

        rows = pl.ds(pl.multiple_of(i * tile, NB), tile)
        left = left_ref[rows, :]

        def products(start):
            cols = slice(start, min(start + NB, width))
            return dot(left[:, :NB], top_ref[:NB, cols]), dot(left[:, NB:], top_ref[NB:, cols])

        ahead = products(0)
        for start in range(0, width, NB):
            cols = slice(start, min(start + NB, width))
            first_change, second_change = ahead
            if start + NB < width:
                ahead = products(start + NB)
            value = reads[slot, :, cols].astype(jnp.float32) + first_change
            value = value.astype(jnp.bfloat16).astype(jnp.float32) + second_change
            writes[slot, :, cols] = value.astype(jnp.bfloat16)

        @pl.when((i == 0) & (grid_row == 0))
        def _():
            writes[slot, :NB, :] = -top_ref[:NB, :]

        @pl.when((i == 0) & (grid_row == 1))
        def _():
            writes[slot, :NB, :] = -top_ref[NB:, :]

        if first == 0:
            @pl.when((j == 0) & (grid_col == 0))
            def _():
                writes[slot, :, :NB] = left_ref[rows, :NB]

            @pl.when((j == 0) & (grid_col == 1))
            def _():
                writes[slot, :, :NB] = left_ref[rows, NB:]

            @pl.when((j == 0) & (i == 0) & (grid_col == 0) & (grid_row == 0))
            def _():
                writes[slot, :NB, :NB] = packed_first[...].astype(jnp.bfloat16)

            @pl.when((j == 0) & (i == 0) & (grid_col == 1) & (grid_row == 0))
            def _():
                writes[slot, :NB, :NB] = -top_ref[:NB, :NB]

            @pl.when((j == 0) & (i == 0) & (grid_col == 1) & (grid_row == 1))
            def _():
                writes[slot, :NB, :NB] = packed_second[...].astype(jnp.bfloat16)

        write(step)
        return carry

    lax.fori_loop(0, steps, body, 0)
    for step in range(steps - SLOTS, steps):
        wait_write(step)


def update_call(first, last, lines, place, matrix, left, squares, left_block, own, other, extra, before):
    rows, cols = matrix.shape
    width = cols // CHUNKS
    tile = rows // ROW_TILES
    count = last - first
    tail = list(extra) + ([] if before is None else [before])
    operands = [place, left, *squares, left_block, matrix, *own, *other, *tail]
    aliases = {} if before is None else {len(operands) - 1: 0}
    return pl.pallas_call(
        functools.partial(update_kernel, first, count, lines, len(tail)),
        out_shape=jax.ShapeDtypeStruct((rows, cols), jnp.bfloat16),
        in_specs=[smem()]
        + [vmem()] * 6
        + [hbm()]
        + [anywhere() for _ in range(len(own) + len(other) + len(extra))]
        + [hbm() for _ in tail[len(extra) :]],
        out_specs=hbm(),
        scratch_shapes=[
            pltpu.VMEM((2, count, NB, width), jnp.bfloat16),
            pltpu.VMEM((2 * NB, width), jnp.bfloat16),
            pltpu.VMEM((2, NB, 2 * NB), jnp.bfloat16),
            pltpu.VMEM((SLOTS, tile, width), jnp.bfloat16),
            pltpu.VMEM((SLOTS, tile, width), jnp.bfloat16),
            pltpu.SemaphoreType.DMA((2, count)),
            pltpu.SemaphoreType.DMA((SLOTS,)),
            pltpu.SemaphoreType.DMA((SLOTS,)),
        ],
        input_output_aliases=aliases,
        compiler_params=pltpu.CompilerParams(vmem_limit_bytes=26 * MIB),
        cost_estimate=pl.CostEstimate(
            flops=6 * rows * NB * width * count,
            bytes_accessed=6 * rows * width * count,
            transcendentals=0,
        ),
    )(*operands)


def swap(size):
    return [(i, i ^ 1) for i in range(size)]


def spread(block, axis, reach, index, size):
    stride = reach // 2
    while stride >= 2:
        pairs = [(i, i + stride) for i in range(size) if i % (2 * stride) < 2]
        moved = lax.ppermute(block, axis, pairs)
        block = jnp.where(index % (2 * stride) >= stride, moved, block)
        stride //= 2
    return block


def on_device(matrix):
    grid_rows = lax.axis_size("row")
    grid_cols = lax.axis_size("col")
    grid_row = lax.axis_index("row")
    grid_col = lax.axis_index("col")
    place = jnp.stack([grid_row, grid_col]).astype(jnp.int32)
    lines = grid_rows // 2
    width = matrix.shape[1] // CHUNKS

    diag = spread(matrix[:NB, :NB], "col", grid_cols, grid_col, grid_cols)
    half = grid_rows // 2
    pairs = [(i, i + half) for i in range(2)]
    diag = jnp.where(grid_row >= half, lax.ppermute(diag, "row", pairs), diag)
    near = diag[:1, :1]
    diag = spread(diag, "row", half, grid_row, grid_rows)
    both_swap = [
        (i * grid_cols + j, (i ^ 1) * grid_cols + (j ^ 1))
        for i in range(grid_rows)
        for j in range(grid_cols)
    ]
    blocks = (
        diag,
        lax.ppermute(diag, "col", swap(grid_cols)),
        lax.ppermute(diag, "row", swap(grid_rows)),
        lax.ppermute(diag, ("row", "col"), both_swap),
    )

    n_ticks = CHUNKS + lines - 1
    own, other, received = [], [], []

    def move(done):
        tick = len(own)
        if tick >= n_ticks:
            return done[:1]
        if tick == 0:
            send = jnp.where(grid_row < 2, matrix[:NB, :width], diag[:1, :1])
        else:
            column = min(tick, CHUNKS - 1) * width
            send = gate_call(column, place, matrix, received[-1], [*other[-2:-1], *done])
        live = [k for k in range(lines) if 0 <= tick - k < CHUNKS]
        onward = [(2 * k + e, 2 * k + 2 + e) for k in live for e in range(2) if k + 1 < lines]
        across = [(2 * k + e, 2 * k + 1 - e) for k in live for e in range(2)]
        received.append(lax.ppermute(send, "row", onward) if onward else send)
        own.append(send)
        other.append(lax.ppermute(send, "row", across))
        return [send]

    move([])
    extra = move(blocks[1:])
    stride = grid_cols // 2
    column = jnp.where(grid_col < 2, matrix[:, :NB], near)
    pairs = [(i, i + stride) for i in range(grid_cols) if i % (2 * stride) < 2]
    moved = lax.ppermute(column, "col", pairs)

    cost = 10**9
    per_piece = NB // W // PIECES
    kept = []
    for section in range(2):
        for piece in range(PIECES):
            if section > 0 and piece == 0:
                extra = move(square[:1])
                moved = hold_call(moved, extra)
                extra = [*extra, moved]
            if piece > 0:
                extra = []
                body = functools.partial(next_kernel, piece * per_piece, per_piece, len(extra))
                square = factor_call(body, 3, None, square, extra, cost)
            elif section == 0:
                body = functools.partial(first_kernel, per_piece, len(extra))
                square = factor_call(body, 3, place, blocks, extra, cost)
            else:
                body = functools.partial(second_kernel, per_piece, len(extra))
                *square, left_block, top_block = factor_call(
                    body, 5, place, [*blocks, *kept[0][1:]], extra, cost
                )
        kept.append(square)

    packed, lower, upper = zip(*kept)
    column = jnp.where(grid_col % (2 * stride) >= stride, moved, column)
    column = spread(column, "col", stride, grid_col, grid_cols)
    column_other = lax.ppermute(column, "col", swap(grid_cols))
    left = left_call(place, column, column_other, *upper, top_block, move(square[:1]))
    latest = left
    out = None
    for first, last in BATCHES:
        while len(own) < min(last + lines, n_ticks):
            latest = move([latest])[0]
        sent = range(first, last + lines - 1)
        out = update_call(
            first, last, lines, place, matrix, left, (*packed, *lower), left_block,
            [own[t] for t in sent], [other[t] for t in sent], [] if latest is out else [latest], out,
        )
        latest = out
    return out


def solution(mesh):
    return jax.shard_map(
        on_device, mesh=mesh, in_specs=(P("row", "col"),), out_specs=P("row", "col"), check_vma=False
    )
```
